256 devices in a mesh: dp: 8 (over z), expert: 8 (over y, core), tensor: 4 (over x).
Axes of the slice: x: 4, y: 4, z: 8, core: 2. Of those that a mesh axis runs over, the one named last changes fastest.
Arguments:
- tokens: bfloat16 [1024, 6144], P('dp', 'expert'), may hold values from -6 to 6
- out_grad: bfloat16 [1024, 6144], P('dp', 'expert'), may hold values from -3 to 3
- expert_ids: int32 [1024, 2], P('dp'), may hold values from 0 to 7, all different within a row; in each aligned block of 128 rows (0 to 127, 128 to 255, ...) at most 48 rows name the same one
- combine_weights: float32 [1024, 2], P('dp'), may hold values from 0.05 to 1
- w_gate: bfloat16 [8, 6144, 8192], P('expert', None, ('dp', 'tensor')), may hold values from -0.078125 to 0.078125
- w_up: bfloat16 [8, 6144, 8192], P('expert', None, ('dp', 'tensor')), may hold values from -0.078125 to 0.078125
- w_down: bfloat16 [8, 8192, 6144], P('expert', ('dp', 'tensor')), may hold values from -0.0625 to 0.0625
Outputs:
- x_grad: bfloat16 [1024, 6144], P('dp', 'expert')
- router_grad: float32 [1024, 2], P('dp')
The draws below stay inside these ranges and needn't reach their ends.
Inputs may be any that keep to these rules, and one draw needn't show every extreme that they name: `expert_ids`: in each aligned block of 128 tokens (the tokens of one index of dp) at most 48 entries name one expert, a bound that the crowded blocks reach; the two experts of a token differ.
All inputs are finite; a program needn't handle non-finite values.
Results may differ from the reference program's by a relative error of at most 0.0049.
Values may be sent and summed in bfloat16 or wider, within the bound.
No kernel may reach another device: no remote copies, remote signals or barrier semaphores. Data moves between devices by JAX's collectives and lax.ppermute only.
A program may use at most 128 MiB of HBM per device.

```python
import math
import jax
import jax.numpy as jnp
import numpy as np
from jax import lax

D = 6144
EXPERTS = 8
FF_W = 8192
TOK_DEV = 128
TOKENS = 1024
CAP = 48
ROWS = 384
N_DP = 8


def level_of(key, extent, pieces, low, largest):
    def one(dim, blocks):
        steps = jax.random.uniform(jax.random.fold_in(jax.random.fold_in(key, 6), dim), (blocks,), jnp.float32, low / len(pieces), largest / len(pieces))
        return jnp.repeat(jnp.exp(steps), extent[dim] // blocks).reshape((-1,) + (1,) * (len(extent) - dim - 1))

    level = one(*pieces[0])
    for cut in pieces[1:]:
        level = level * one(*cut)
    return level


def deal_out(own_key, own, number, rows, count, top, limit, lean):
    ranking = jax.random.permutation(own_key, count)
    heavy_load, usual = load_shares(count, rows * top, limit, lean, True), load_shares(count, rows * top, limit, lean, False)
    places = jnp.arange(count)

    def named(sizes, rotation):
        used = int((sizes > 0).sum())
        fixed = max(1, used // 4)
        moved = fixed + (places - fixed + rotation * (used - fixed)) % max(1, count - fixed)
        return jnp.zeros((count,), jnp.int32).at[ranking[jnp.where(places < fixed, places, moved)]].set(jnp.asarray(sizes, jnp.int32))

    sizes = jnp.where(number % 4 == 0, named(heavy_load, number // 4), named(usual, number - number // 4 - 1))
    mixed = jax.random.permutation(jax.random.fold_in(own, 3), count)
    donor, sink = mixed[0:count // 2 * 2:2], mixed[1:count // 2 * 2:2]
    room = jnp.minimum(sizes[donor] - 1, limit - sizes[sink]) // 2
    room = jnp.where((donor == ranking[0]) | (sink == ranking[0]) | (sizes[sink] == 0), 0, jnp.maximum(room, 0))
    moved = jax.random.randint(jax.random.fold_in(own, 4), (count // 2,), 0, 1 << 20) % (room + 1)
    sizes = sizes.at[donor].add(-moved).at[sink].add(moved)
    items = jnp.searchsorted(jnp.cumsum(sizes), jnp.arange(rows * top), side="right").astype(jnp.int32)
    grid = items.reshape(top, rows).T
    grid = grid[jax.random.permutation(jax.random.fold_in(own, 1), rows)]
    rotation = jax.random.randint(jax.random.fold_in(own, 2), (rows, 1), 0, top)
    return jnp.take_along_axis(grid, (jnp.arange(top)[None, :] + rotation) % top, axis=1)


def load_shares(amount, total, reach, lean, full):
    weights = [(1 << 20) // math.isqrt(grade ** lean) + 1 for grade in range(1, amount + 1)]
    largest = reach if full else min(reach, max(-(-total // amount), total * weights[0] // sum(weights)))
    least = 1 if total - largest >= amount - 1 else 0
    given, surplus = [largest] + [least] * (amount - 1), total - largest - least * (amount - 1)
    while surplus > 0:
        candidates = [i for i in range(1, amount) if given[i] < largest] or [i for i in range(1, amount) if given[i] < reach]
        pool, remaining = sum([weights[i] for i in candidates]), surplus
        for i in candidates:
            more = min(reach - given[i], max(1, remaining * weights[i] // pool), surplus)
            given[i] = given[i] + more
            surplus = surplus - more
    return np.array(given)


def noise(rng, shape, scale, limit, split=(), kind=jnp.bfloat16):
    result = scale * jax.random.normal(rng, shape, jnp.float32)
    if split:
        result = result * level_of(rng, shape, split, -0.22, 0.18)
    return jnp.clip(result, -limit, limit).astype(kind)


def setup_inputs(seed: int = 0) -> dict:
    streams_of = jax.random.split(jax.random.key(seed), 8)
    tokens = noise(streams_of[0], (TOKENS, D), 1.0, 6.0, ((0, 8), (1, 8)))
    out_grad = noise(streams_of[1], (TOKENS, D), 0.5, 3.0, ((0, 8), (1, 8)))
    expert_ids_keys = jax.random.split(jax.random.fold_in(streams_of[2], 1), TOKENS // TOK_DEV)
    expert_ids_turns = jax.random.permutation(jax.random.fold_in(streams_of[2], 3), TOKENS // TOK_DEV)
    expert_ids = jax.vmap(lambda own, number: deal_out(jax.random.fold_in(streams_of[2], 2), own, number, TOK_DEV, EXPERTS, 2, CAP, 2))(expert_ids_keys, expert_ids_turns).reshape((TOKENS, 2))
    combine_weights = jnp.clip(0.05 + 0.95 * jax.random.uniform(streams_of[3], (TOKENS, 2), jnp.float32) ** level_of(streams_of[3], (TOKENS, 2), ((0, 8),), -0.2, 0.2), 0.05, 1.0)
    w_gate = noise(streams_of[4], (EXPERTS, D, FF_W), D ** -0.5, 0.078125, ((0, 8), (2, 32)))
    w_up = noise(streams_of[5], (EXPERTS, D, FF_W), D ** -0.5, 0.078125, ((0, 8), (2, 32)))
    w_down = noise(streams_of[6], (EXPERTS, FF_W, D), FF_W ** -0.5, 0.0625, ((0, 8), (1, 32)))
    return dict(tokens=tokens, out_grad=out_grad, expert_ids=expert_ids, combine_weights=combine_weights, w_gate=w_gate, w_up=w_up, w_down=w_down)


def reference(tokens, out_grad, expert_ids, combine_weights, w_gate, w_up, w_down):
    token_count = tokens.shape[0]
    block_ids = expert_ids.reshape(N_DP, TOK_DEV * 2)
    expert_range = jnp.arange(EXPERTS, dtype=jnp.int32)
    one_hot = (block_ids[:, :, None] == expert_range[None, None, :]).astype(jnp.int32)
    earlier = jnp.cumsum(one_hot, axis=1).astype(jnp.int32) - one_hot
    slot_index = jnp.sum(earlier * one_hot, axis=2).astype(jnp.int32)
    block_start = (jnp.arange(N_DP, dtype=jnp.int32) * CAP)[:, None]
    buffer_row = (block_start + slot_index).reshape(-1).astype(jnp.int32)
    flat_ids = expert_ids.reshape(-1)
    token_index = jnp.arange(token_count * 2, dtype=jnp.int32) // 2
    row_table = jnp.full((EXPERTS, ROWS), token_count, jnp.int32).at[flat_ids, buffer_row].set(token_index)
    zero_row = jnp.zeros((1, D), tokens.dtype)
    padded_input = jnp.concatenate([tokens, zero_row], axis=0)
    padded_cotangent = jnp.concatenate([out_grad, zero_row], axis=0)

    def one_expert(operands):
        table_rows, gate_matrix, up_matrix, down_matrix = operands
        inputs = padded_input[table_rows]
        cotangents = padded_cotangent[table_rows]
        gate_value = jnp.dot(inputs, gate_matrix, preferred_element_type=jnp.float32)
        up_value = jnp.dot(inputs, up_matrix, preferred_element_type=jnp.float32)
        sigmoid_gate = jax.nn.sigmoid(gate_value)
        activation = gate_value * sigmoid_gate
        hidden_value = activation * up_value
        backward = jnp.dot(cotangents, down_matrix.T, preferred_element_type=jnp.float32)
        slot_grad = jnp.sum(backward * hidden_value, axis=1)
        grad_up = (backward * activation).astype(jnp.bfloat16)
        grad_gate = (backward * up_value * sigmoid_gate * (1.0 + gate_value * (1.0 - sigmoid_gate))).astype(jnp.bfloat16)
        input_grad = jnp.dot(grad_gate, gate_matrix.T, preferred_element_type=jnp.float32)
        input_grad = input_grad + jnp.dot(grad_up, up_matrix.T, preferred_element_type=jnp.float32)
        return input_grad, slot_grad

    input_grad, slot_grad = lax.map(one_expert, (row_table, w_gate, w_up, w_down))
    picked = input_grad[flat_ids, buffer_row] * combine_weights.reshape(-1)[:, None]
    x_grad = jnp.sum(picked.reshape(token_count, 2, D), axis=1).astype(jnp.bfloat16)
    router_grad = slot_grad[flat_ids, buffer_row].reshape(token_count, 2)
    return x_grad, router_grad
```

```python
import functools

import jax
import jax.numpy as jnp
from jax import lax
from jax.experimental import pallas as pl
from jax.experimental.pallas import tpu as pltpu
from jax.sharding import PartitionSpec as P

EXPERTS = 8
CAP = 48
BF = jnp.bfloat16
F32 = jnp.float32
HIGH = lax.Precision.HIGHEST


def nt(a, b, **kw):
    return lax.dot_general(a, b, (((1,), (1,)), ((), ())), preferred_element_type=F32, **kw)


def tn(a, b, **kw):
    return lax.dot_general(a, b, (((0,), (0,)), ((), ())), preferred_element_type=F32, **kw)


def slot_masks(ids):
    tokens = ids.shape[1]
    experts = lax.broadcasted_iota(jnp.int32, (EXPERTS, tokens), 0)
    ind0 = (ids[0:1, :] == experts).astype(F32)
    ind1 = (ids[1:2, :] == experts).astype(F32)
    before = (
        lax.broadcasted_iota(jnp.int32, (tokens, tokens), 0)
        < lax.broadcasted_iota(jnp.int32, (tokens, tokens), 1)
    )
    count = jnp.dot((ind0 + ind1).astype(BF), before.astype(BF), preferred_element_type=F32)
    return ind0, ind1, count.astype(jnp.int32)


def dispatch_kernel(ids_ref, tok_ref, og_ref, out_ref):
    ind0, ind1, count = slot_masks(ids_ref[...])
    ind = ind0 + ind1
    tokens = ind.shape[1]
    slots = lax.broadcasted_iota(jnp.int32, (CAP, tokens), 0)
    for e in range(EXPERTS):
        pick = jnp.where(count[e : e + 1, :] == slots, ind[e : e + 1, :], 0.0).astype(BF)
        out_ref[e, 0:CAP, :] = jnp.dot(pick, tok_ref[...], preferred_element_type=F32).astype(BF)
        out_ref[e, CAP : 2 * CAP, :] = jnp.dot(
            pick, og_ref[...], preferred_element_type=F32
        ).astype(BF)


def dispatch(ids, tokens, out_grad):
    width = tokens.shape[1]
    return pl.pallas_call(
        dispatch_kernel,
        out_shape=jax.ShapeDtypeStruct((EXPERTS, 2 * CAP, width), BF),
        compiler_params=pltpu.CompilerParams(vmem_limit_bytes=24 << 20),
        name="dispatch",
    )(ids, tokens, out_grad)


def forward_kernel(count, halves, *refs):
    n_in = 2 if halves else count
    ins = refs[:n_in]
    wg_ref, wu_ref, wd_ref = refs[n_in : n_in + 3]
    outs = refs[n_in + 3 : n_in + 3 + 2 * count]
    acc_g, acc_u, acc_b = refs[n_in + 3 + 2 * count :]
    e = pl.program_id(0)

    @pl.when(e == 0)
    def _():
        acc_g[...] = jnp.zeros_like(acc_g)
        acc_u[...] = jnp.zeros_like(acc_u)
        acc_b[...] = jnp.zeros_like(acc_b)

    if halves:
        blocks = [jnp.where(e < EXPERTS // 2, ins[0][0], ins[1][0])]
    else:
        blocks = [r[0] for r in ins]
    tok = jnp.concatenate([b[:CAP] for b in blocks], axis=0)
    og = jnp.concatenate([b[CAP:] for b in blocks], axis=0)
    acc_g[...] += jnp.dot(tok, wg_ref[0], preferred_element_type=F32)
    acc_u[...] += jnp.dot(tok, wu_ref[0], preferred_element_type=F32)
    acc_b[...] += nt(og, wd_ref[0])

    @pl.when(e == EXPERTS - 1)
    def _():
        gate, up, back = acc_g[...], acc_u[...], acc_b[...]
        sig = jax.nn.sigmoid(gate)
        act = gate * sig
        prod = back * (act * up)
        grad_up = (back * act).astype(BF)
        grad_gate = (back * up * sig * (1.0 + gate * (1.0 - sig))).astype(BF)
        hidden = gate.shape[1]
        ones = jnp.ones((16, hidden), F32)
        fill = jnp.zeros((128 - CAP, hidden), F32)
        for i in range(count):
            rows = slice(i * CAP, (i + 1) * CAP)
            outs[2 * i][:, :hidden] = grad_gate[rows]
            outs[2 * i][:, hidden:] = grad_up[rows]
            outs[2 * i + 1][...] = nt(
                ones, jnp.concatenate([prod[rows], fill], axis=0), precision=HIGH
            )


def forward(blocks, halves, w_gate, w_up, w_down):
    hidden = w_gate.shape[2]
    width = blocks[0].shape[2]
    count = 1 if halves else len(blocks)
    shape = (1, 2 * CAP, width)
    if halves:
        last = EXPERTS // 2 - 1
        in_specs = [
            pl.BlockSpec(shape, lambda e: (jnp.minimum(e, last), 0, 0)),
            pl.BlockSpec(shape, lambda e: (jnp.maximum(e - last - 1, 0), 0, 0)),
        ]
    else:
        in_specs = [pl.BlockSpec(shape, lambda e: (e, 0, 0)) for _ in blocks]
    in_specs += [
        pl.BlockSpec((1, width, hidden), lambda e: (0, e, 0)),
        pl.BlockSpec((1, width, hidden), lambda e: (0, e, 0)),
        pl.BlockSpec((1, hidden, width), lambda e: (0, 0, e)),
    ]
    rows = count * CAP
    outs = pl.pallas_call(
        functools.partial(forward_kernel, count, halves),
        grid=(EXPERTS,),
        in_specs=in_specs,
        out_specs=[
            pl.BlockSpec((CAP, 2 * hidden), lambda e: (0, 0)),
            pl.BlockSpec((16, 128), lambda e: (0, 0)),
        ]
        * count,
        out_shape=[
            jax.ShapeDtypeStruct((CAP, 2 * hidden), BF),
            jax.ShapeDtypeStruct((16, 128), F32),
        ]
        * count,
        scratch_shapes=[pltpu.VMEM((rows, hidden), F32)] * 3,
        compiler_params=pltpu.CompilerParams(vmem_limit_bytes=24 << 20),
        cost_estimate=pl.CostEstimate(
            flops=6 * 256 * EXPERTS * width * hidden,
            bytes_accessed=6 * EXPERTS * width * hidden,
            transcendentals=0,
        ),
        name="forward",
    )(*blocks, w_gate, w_up, w_down)
    return [(outs[2 * i], outs[2 * i + 1]) for i in range(count)]


def pack_slots(total, width):
    high = total.astype(BF).astype(F32)
    low = total - high
    row = lax.broadcasted_iota(jnp.int32, (16, 128), 0)
    packed = jnp.where(row == 0, high, jnp.where(row == 1, low, 0.0)).astype(BF)
    return jnp.concatenate([packed, jnp.zeros((16, width - 128), BF)], axis=1)


def unpack_slots(rows):
    packed = rows.astype(F32)
    return packed[0:1] + packed[1:2]


def backward_kernel(dist, *refs):
    e = pl.program_id(0)
    half = EXPERTS // 2
    if dist == 4:
        g_ref, s_ref, wg_ref, wu_ref, plus_ref, minus_ref = refs
    elif dist == 0:
        g_ref, s_ref, rp_ref, rm_ref, wg_ref, wu_ref, out_ref = refs
    else:
        gp_ref, sp_ref, gm_ref, sm_ref, rp_ref, rm_ref, wg_ref, wu_ref, plus_ref, minus_ref = refs
    hidden = wg_ref.shape[2]
    width = wg_ref.shape[1]

    def product(grads):
        return nt(grads[:, :hidden], wg_ref[0]) + nt(grads[:, hidden:], wu_ref[0])

    if dist == 4:
        part = product(g_ref[...]).astype(BF)

        @pl.when(e == 0)
        def _():
            plus_ref[0:16, :] = pack_slots(s_ref[0:1, :], width)

        @pl.when(e < half)
        def _():
            plus_ref[pl.ds(pl.multiple_of(16 + e * CAP, 16), CAP), :] = part

        @pl.when(e >= half)
        def _():
            minus_ref[pl.ds(pl.multiple_of((e - half) * CAP, 16), CAP), :] = part

    elif dist == 3:
        part = product(jnp.concatenate([gp_ref[...], gm_ref[...]], axis=0))
        place = pl.ds(pl.multiple_of(16 + e * CAP, 16), CAP)

        @pl.when(e == 0)
        def _():
            plus_ref[0:16, :] = pack_slots(
                sp_ref[0:1, :] + unpack_slots(rp_ref[0:16, 0:128]), width
            )
            minus_ref[0:16, :] = pack_slots(sm_ref[0:1, :], width)

        @pl.when(e < half)
        def _():
            plus_ref[place, :] = (part[:CAP] + rp_ref[place, :].astype(F32)).astype(BF)
            minus_ref[place, :] = part[CAP:].astype(BF)

        @pl.when(e >= half)
        def _():
            from_minus = rm_ref[pl.ds(pl.multiple_of((e - half) * CAP, 16), CAP), :].astype(F32)
            plus_ref[place, :] = part[:CAP].astype(BF)
            minus_ref[place, :] = (part[CAP:] + from_minus).astype(BF)

    elif dist == 0:
        place = pl.ds(pl.multiple_of(16 + e * CAP, 16), CAP)
        part = product(g_ref[...])
        part = part + (rp_ref[place, :].astype(F32) + rm_ref[place, :].astype(F32))
        out_ref[0, 0:CAP, :] = part.astype(BF)
        total = s_ref[0:1, :] + (
            unpack_slots(rp_ref[0:16, 0:128]) + unpack_slots(rm_ref[0:16, 0:128])
        )
        out_ref[0, CAP : CAP + 16, :] = pack_slots(total, width)
    else:
        part = product(jnp.concatenate([gp_ref[...], gm_ref[...]], axis=0))
        place = pl.ds(pl.multiple_of(16 + e * CAP, 16), CAP)

        @pl.when(e == 0)
        def _():
            plus_ref[0:16, :] = pack_slots(
                sp_ref[0:1, :] + unpack_slots(rp_ref[0:16, 0:128]), width
            )
            minus_ref[0:16, :] = pack_slots(
                sm_ref[0:1, :] + unpack_slots(rm_ref[0:16, 0:128]), width
            )

        plus_ref[place, :] = (part[:CAP] + rp_ref[place, :].astype(F32)).astype(BF)
        minus_ref[place, :] = (part[CAP:] + rm_ref[place, :].astype(F32)).astype(BF)


def backward(dist, small, received, w_gate, w_up):
    hidden = w_gate.shape[2]
    width = w_gate.shape[1] // EXPERTS
    half_rows = CAP * EXPERTS // 2
    full = 16 + CAP * EXPERTS

    def whole(a):
        return pl.BlockSpec(a.shape, lambda e: (0,) * len(a.shape))

    if dist == 4:
        shapes = [(16 + half_rows, width), (half_rows, width)]
    elif dist == 0:
        shapes = [(EXPERTS, CAP + 16, width)]
    else:
        shapes = [(full, width), (full, width)]
    out_shape = [jax.ShapeDtypeStruct(s, BF) for s in shapes]
    if dist == 0:
        out_specs = [pl.BlockSpec((1, CAP + 16, width), lambda e: (e, 0, 0))]
    else:
        out_specs = [whole(s) for s in out_shape]
    return pl.pallas_call(
        functools.partial(backward_kernel, dist),
        grid=(EXPERTS,),
        in_specs=[whole(a) for a in (*small, *received)]
        + [pl.BlockSpec((1, width, hidden), lambda e: (0, e, 0))] * 2,
        out_specs=out_specs,
        out_shape=out_shape,
        compiler_params=pltpu.CompilerParams(vmem_limit_bytes=24 << 20),
        cost_estimate=pl.CostEstimate(
            flops=4 * 256 * EXPERTS * width * hidden,
            bytes_accessed=4 * EXPERTS * width * hidden,
            transcendentals=0,
        ),
        name="backward",
    )(*small, *received, w_gate, w_up)


def combine_kernel(ids_ref, weight_ref, rows_ref, out_ref):
    ind0, ind1, count = slot_masks(ids_ref[...])
    tokens = ind0.shape[1]
    width = rows_ref.shape[2]
    weights = weight_ref[...]
    scale = ind0 * weights[0:1, :] + ind1 * weights[1:2, :]
    slots = lax.broadcasted_iota(jnp.int32, (CAP, tokens), 0)
    total = jnp.zeros((tokens, width), F32)
    router0 = jnp.zeros((16, tokens), F32)
    router1 = jnp.zeros((16, tokens), F32)
    for e in range(EXPERTS):
        here = count[e : e + 1, :] == slots
        pick = jnp.where(here, scale[e : e + 1, :], 0.0)
        total += tn(pick, rows_ref[e, 0:CAP, :].astype(F32), precision=HIGH)
        slot_rows = rows_ref[e, CAP : CAP + 16, 0:128][:, :CAP].astype(F32)
        one0 = jnp.where(here, ind0[e : e + 1, :], 0.0)
        one1 = jnp.where(here, ind1[e : e + 1, :], 0.0)
        router0 += jnp.dot(slot_rows, one0, precision=HIGH, preferred_element_type=F32)
        router1 += jnp.dot(slot_rows, one1, precision=HIGH, preferred_element_type=F32)
    out_ref[0:tokens, :] = total.astype(BF)
    sum0 = router0[0:1] + router0[1:2]
    sum1 = router1[0:1] + router1[1:2]
    high0, high1 = sum0.astype(BF).astype(F32), sum1.astype(BF).astype(F32)
    row = lax.broadcasted_iota(jnp.int32, (16, tokens), 0)
    packed = jnp.where(row == 0, high0, 0.0) + jnp.where(row == 1, sum0 - high0, 0.0)
    packed = packed + jnp.where(row == 2, high1, 0.0) + jnp.where(row == 3, sum1 - high1, 0.0)
    out_ref[tokens : tokens + 16, :] = jnp.concatenate(
        [packed.astype(BF), jnp.zeros((16, width - tokens), BF)], axis=1
    )


def combine(ids, weights, rows):
    tokens = ids.shape[1]
    return pl.pallas_call(
        combine_kernel,
        out_shape=jax.ShapeDtypeStruct((tokens + 16, rows.shape[2]), BF),
        compiler_params=pltpu.CompilerParams(vmem_limit_bytes=24 << 20),
        name="combine",
    )(ids, weights, rows)


def finish_kernel(a_ref, b_ref, c_ref, d_ref, x_ref, r_ref):
    tokens = x_ref.shape[0]
    total = (a_ref[...].astype(F32) + c_ref[...].astype(F32)) + (
        b_ref[...].astype(F32) + d_ref[...].astype(F32)
    )
    x_ref[...] = total[:tokens].astype(BF)
    tail = total[tokens : tokens + 16, :tokens]
    r_ref[0:1, :] = tail[0:1] + tail[1:2]
    r_ref[1:2, :] = tail[2:3] + tail[3:4]


def finish(own, plus, two, minus):
    tokens = own.shape[0] - 16
    return pl.pallas_call(
        finish_kernel,
        out_shape=(
            jax.ShapeDtypeStruct((tokens, own.shape[1]), BF),
            jax.ShapeDtypeStruct((2, tokens), F32),
        ),
        compiler_params=pltpu.CompilerParams(vmem_limit_bytes=24 << 20),
        name="finish",
    )(own, plus, two, minus)


def shift(a, axis, by):
    n = lax.axis_size(axis)
    return lax.ppermute(a, axis, [(i, (i + by) % n) for i in range(n)])


def per_device(tokens, out_grad, expert_ids, combine_weights, w_gate, w_up, w_down):
    ids = expert_ids.T
    weights = combine_weights.T
    half = EXPERTS // 2
    send = dispatch(ids, tokens, out_grad)
    own = lax.all_to_all(send, "expert", split_axis=0, concat_axis=0)
    up, down = own, own
    grads = {}
    blocks = {0: [own]}
    for dist in range(1, 4):
        up, down = shift(up, "dp", 1), shift(down, "dp", -1)
        blocks[dist] = [down, up]
    blocks[4] = [shift(up[:half], "dp", 1), shift(down[half:], "dp", -1)]
    for dist in range(5):
        grads[dist] = forward(blocks[dist], dist == 4, w_gate, w_up, w_down)
    received = ()
    for dist in range(4, 0, -1):
        small = [a for pair in grads[dist] for a in pair]
        plus, minus = backward(dist, small, received, w_gate, w_up)
        received = (shift(plus, "dp", 1), shift(minus, "dp", -1))
    (rows,) = backward(0, list(grads[0][0]), received, w_gate, w_up)
    rows = lax.all_to_all(rows, "expert", split_axis=0, concat_axis=0)
    part = combine(ids, weights, rows)
    x_grad, router = finish(
        part, shift(part, "tensor", 1), shift(part, "tensor", 2), shift(part, "tensor", -1)
    )
    return x_grad, router.T


def solution(mesh):
    placed = (
        P("dp", "expert"),
        P("dp", "expert"),
        P("dp", None),
        P("dp", None),
        P("expert", None, ("dp", "tensor")),
        P("expert", None, ("dp", "tensor")),
        P("expert", ("dp", "tensor"), None),
    )
    return jax.shard_map(
        per_device,
        mesh=mesh,
        in_specs=placed,
        out_specs=(P("dp", "expert"), P("dp", None)),
        check_vma=False,
    )
```

```python
import functools

import jax
import jax.numpy as jnp
from jax import lax
from jax.experimental import pallas as pl
from jax.experimental.pallas import tpu as pltpu
from jax.sharding import PartitionSpec as P

EXPERTS = 8
CAP = 48
WHOLE = 256
PART = 128
BF = jnp.bfloat16
F32 = jnp.float32
HIGH = lax.Precision.HIGHEST


def nt(a, b, **kw):
    return lax.dot_general(a, b, (((1,), (1,)), ((), ())), preferred_element_type=F32, **kw)


def tn(a, b, **kw):
    return lax.dot_general(a, b, (((0,), (0,)), ((), ())), preferred_element_type=F32, **kw)


def slot_masks(ids):
    tokens = ids.shape[1]
    experts = lax.broadcasted_iota(jnp.int32, (EXPERTS, tokens), 0)
    ind0 = (ids[0:1, :] == experts).astype(F32)
    ind1 = (ids[1:2, :] == experts).astype(F32)
    before = (
        lax.broadcasted_iota(jnp.int32, (tokens, tokens), 0)
        < lax.broadcasted_iota(jnp.int32, (tokens, tokens), 1)
    )
    count = jnp.dot((ind0 + ind1).astype(BF), before.astype(BF), preferred_element_type=F32)
    return ind0, ind1, count.astype(jnp.int32)


def dispatch_kernel(place_ref, ids_ref, tok_ref, og_ref, out_ref):
    ind0, ind1, count = slot_masks(ids_ref[...])
    ind = ind0 + ind1
    tokens = ind.shape[1]
    slots = lax.broadcasted_iota(jnp.int32, (CAP, tokens), 0)
    quarter = pl.ds(pl.multiple_of(WHOLE + place_ref[1] * PART, 128), PART)
    tok, og = tok_ref[:, 0:WHOLE], og_ref[:, 0:WHOLE]
    tok_part, og_part = tok_ref[:, quarter], og_ref[:, quarter]
    for e in range(EXPERTS):
        pick = jnp.where(count[e : e + 1, :] == slots, ind[e : e + 1, :], 0.0).astype(BF)
        column = 0
        for source in (tok, og, tok_part, og_part):
            width = source.shape[1]
            out_ref[e, :, column : column + width] = jnp.dot(
                pick, source, preferred_element_type=F32
            ).astype(BF)
            column += width


def dispatch(place, ids, tokens, out_grad):
    return pl.pallas_call(
        dispatch_kernel,
        in_specs=[pl.BlockSpec(memory_space=pltpu.SMEM)]
        + [pl.BlockSpec(memory_space=pltpu.VMEM)] * 3,
        out_shape=jax.ShapeDtypeStruct((EXPERTS, CAP, 2 * (WHOLE + PART)), BF),
        compiler_params=pltpu.CompilerParams(vmem_limit_bytes=24 << 20),
        name="dispatch",
    )(place, ids, tokens, out_grad)


def pieces_near(refs, e):
    own, s_ref, p_ref, m_ref, hd_ref, hu_ref = refs[:4], *refs[4:]
    found = [[r[0] for r in own]]
    for i in range(4):
        two = hd_ref[i, 0] if i < 2 else hu_ref[i - 2, 0]
        found.append([s_ref[i, 0], p_ref[i, 0], m_ref[i, 0], two])
    return found


def pieces_far(refs, e):
    s_ref, p_ref, m_ref, hd_ref, hu_ref = refs
    late = e // (EXPERTS // 2)
    found = []
    for first, step in ((0, 1), (3, 1), (2, 3)):
        i = first + step * late
        if first == 0:
            two = hd_ref[late, 0]
        elif first == 3:
            two = hu_ref[late, 0]
        else:
            two = jnp.where(late == 0, hd_ref[2, 0], hu_ref[2, 0])
        found.append([s_ref[i, 0], p_ref[i, 0], m_ref[i, 0], two])
    return found


def forward_kernel(pieces, count, n_parts, place_ref, *refs):
    whole = refs[:count]
    parts = refs[count : count + n_parts]
    rest = refs[count + n_parts :]
    wg_ref, wu_ref, wd_ref = rest[:3]
    outs = rest[3 : 3 + 2 * count]
    acc_g, acc_u, acc_b, tok_ref, og_ref = rest[3 + 2 * count :]
    e = pl.program_id(0)
    x = place_ref[1]

    @pl.when(e == 0)
    def _():
        acc_g[...] = jnp.zeros_like(acc_g)
        acc_u[...] = jnp.zeros_like(acc_u)
        acc_b[...] = jnp.zeros_like(acc_b)

    for i, found in enumerate(pieces(parts, e)):
        rows = slice(i * CAP, (i + 1) * CAP)
        tok_ref[rows, 0:WHOLE] = whole[i][0, 0, :, 0:WHOLE]
        og_ref[rows, 0:WHOLE] = whole[i][0, 0, :, WHOLE : 2 * WHOLE]
        for piece, offset in zip(found, (0, 3, 1, 2)):
            there = lax.rem(x + offset, 4)
            columns = pl.ds(pl.multiple_of(WHOLE + there * PART, 128), PART)
            tok_ref[rows, columns] = piece[:, 0:PART]
            og_ref[rows, columns] = piece[:, PART : 2 * PART]
    tok = tok_ref[...]
    acc_g[...] += jnp.dot(tok, wg_ref[0], preferred_element_type=F32)
    acc_u[...] += jnp.dot(tok, wu_ref[0], preferred_element_type=F32)
    acc_b[...] += nt(og_ref[...], wd_ref[0])

    @pl.when(e == EXPERTS - 1)
    def _():
        gate, up, back = acc_g[...], acc_u[...], acc_b[...]
        sig = jax.nn.sigmoid(gate)
        act = gate * sig
        prod = back * (act * up)
        grad_up = (back * act).astype(BF)
        grad_gate = (back * up * sig * (1.0 + gate * (1.0 - sig))).astype(BF)
        hidden = gate.shape[1]
        ones = jnp.ones((16, hidden), F32)
        fill = jnp.zeros((128 - CAP, hidden), F32)
        for i in range(count):
            rows = slice(i * CAP, (i + 1) * CAP)
            outs[2 * i][:, :hidden] = grad_gate[rows]
            outs[2 * i][:, hidden:] = grad_up[rows]
            outs[2 * i + 1][...] = nt(
                ones, jnp.concatenate([prod[rows], fill], axis=0), precision=HIGH
            )


def forward(pieces, dists, place, whole, parts, w_gate, w_up, w_down):
    hidden = w_gate.shape[2]
    width = w_gate.shape[1] // EXPERTS
    count = len(dists)
    n_dp = whole.shape[0]

    def whole_spec(dist):
        return pl.BlockSpec(
            (1, 1, CAP, 2 * WHOLE), lambda e, at: (lax.rem(at[0] + dist, n_dp), e, 0, 0)
        )

    def part_spec(a):
        if a.ndim == 3:
            return pl.BlockSpec((1, CAP, 2 * PART), lambda e, at: (e, 0, 0))
        length = a.shape[1]
        return pl.BlockSpec(
            (a.shape[0], 1, CAP, 2 * PART), lambda e, at: (0, lax.rem(e, length), 0, 0)
        )

    in_specs = [whole_spec(dist % n_dp) for dist in dists] + [part_spec(a) for a in parts]
    in_specs += [
        pl.BlockSpec((1, width, hidden), lambda e, at: (0, e, 0)),
        pl.BlockSpec((1, width, hidden), lambda e, at: (0, e, 0)),
        pl.BlockSpec((1, hidden, width), lambda e, at: (0, 0, e)),
    ]
    rows = count * CAP
    outs = pl.pallas_call(
        functools.partial(forward_kernel, pieces, count, len(parts)),
        grid_spec=pltpu.PrefetchScalarGridSpec(
            num_scalar_prefetch=1,
            grid=(EXPERTS,),
            in_specs=in_specs,
            out_specs=[
                pl.BlockSpec((CAP, 2 * hidden), lambda e, at: (0, 0)),
                pl.BlockSpec((16, 128), lambda e, at: (0, 0)),
            ]
            * count,
            scratch_shapes=[pltpu.VMEM((rows, hidden), F32)] * 3
            + [pltpu.VMEM((rows, width), BF)] * 2,
        ),
        out_shape=[
            jax.ShapeDtypeStruct((CAP, 2 * hidden), BF),
            jax.ShapeDtypeStruct((16, 128), F32),
        ]
        * count,
        compiler_params=pltpu.CompilerParams(vmem_limit_bytes=24 << 20),
        cost_estimate=pl.CostEstimate(
            flops=6 * 256 * EXPERTS * width * hidden,
            bytes_accessed=6 * EXPERTS * width * hidden,
            transcendentals=0,
        ),
        name="forward",
    )(place, *([whole] * count), *parts, w_gate, w_up, w_down)
    return [(outs[2 * i], outs[2 * i + 1]) for i in range(count)]


def pack_slots(total, width):
    high = total.astype(BF).astype(F32)
    low = total - high
    row = lax.broadcasted_iota(jnp.int32, (16, 128), 0)
    packed = jnp.where(row == 0, high, jnp.where(row == 1, low, 0.0)).astype(BF)
    return jnp.concatenate([packed, jnp.zeros((16, width - 128), BF)], axis=1)


def unpack_slots(rows):
    packed = rows.astype(F32)
    return packed[0:1] + packed[1:2]


def backward_kernel(dist, *refs):
    e = pl.program_id(0)
    half = EXPERTS // 2
    if dist == 4:
        g_ref, s_ref, wg_ref, wu_ref, plus_ref, minus_ref = refs
    elif dist == 0:
        g_ref, s_ref, rp_ref, rm_ref, wg_ref, wu_ref, out_ref = refs
    else:
        gp_ref, sp_ref, gm_ref, sm_ref, rp_ref, rm_ref, wg_ref, wu_ref, plus_ref, minus_ref = refs
    hidden = wg_ref.shape[2]
    width = wg_ref.shape[1]

    def product(grads):
        return nt(grads[:, :hidden], wg_ref[0]) + nt(grads[:, hidden:], wu_ref[0])

    if dist == 4:
        part = product(g_ref[...]).astype(BF)

        @pl.when(e == 0)
        def _():
            plus_ref[0:16, :] = pack_slots(s_ref[0:1, :], width)

        @pl.when(e < half)
        def _():
            plus_ref[pl.ds(pl.multiple_of(16 + e * CAP, 16), CAP), :] = part

        @pl.when(e >= half)
        def _():
            minus_ref[pl.ds(pl.multiple_of((e - half) * CAP, 16), CAP), :] = part

    elif dist == 3:
        part = product(jnp.concatenate([gp_ref[...], gm_ref[...]], axis=0))
        place = pl.ds(pl.multiple_of(16 + e * CAP, 16), CAP)

        @pl.when(e == 0)
        def _():
            plus_ref[0:16, :] = pack_slots(
                sp_ref[0:1, :] + unpack_slots(rp_ref[0:16, 0:128]), width
            )
            minus_ref[0:16, :] = pack_slots(sm_ref[0:1, :], width)

        @pl.when(e < half)
        def _():
            plus_ref[place, :] = (part[:CAP] + rp_ref[place, :].astype(F32)).astype(BF)
            minus_ref[place, :] = part[CAP:].astype(BF)

        @pl.when(e >= half)
        def _():
            from_minus = rm_ref[pl.ds(pl.multiple_of((e - half) * CAP, 16), CAP), :].astype(F32)
            plus_ref[place, :] = part[:CAP].astype(BF)
            minus_ref[place, :] = (part[CAP:] + from_minus).astype(BF)

    elif dist == 0:
        place = pl.ds(pl.multiple_of(16 + e * CAP, 16), CAP)
        part = product(g_ref[...])
        part = part + (rp_ref[place, :].astype(F32) + rm_ref[place, :].astype(F32))
        out_ref[0, 0:CAP, :] = part.astype(BF)
        total = s_ref[0:1, :] + (
            unpack_slots(rp_ref[0:16, 0:128]) + unpack_slots(rm_ref[0:16, 0:128])
        )
        out_ref[0, CAP : CAP + 16, :] = pack_slots(total, width)
    else:
        part = product(jnp.concatenate([gp_ref[...], gm_ref[...]], axis=0))
        place = pl.ds(pl.multiple_of(16 + e * CAP, 16), CAP)

        @pl.when(e == 0)
        def _():
            plus_ref[0:16, :] = pack_slots(
                sp_ref[0:1, :] + unpack_slots(rp_ref[0:16, 0:128]), width
            )
            minus_ref[0:16, :] = pack_slots(
                sm_ref[0:1, :] + unpack_slots(rm_ref[0:16, 0:128]), width
            )

        plus_ref[place, :] = (part[:CAP] + rp_ref[place, :].astype(F32)).astype(BF)
        minus_ref[place, :] = (part[CAP:] + rm_ref[place, :].astype(F32)).astype(BF)


def backward(dist, small, received, w_gate, w_up):
    hidden = w_gate.shape[2]
    width = w_gate.shape[1] // EXPERTS
    half_rows = CAP * EXPERTS // 2
    full = 16 + CAP * EXPERTS

    def whole(a):
        return pl.BlockSpec(a.shape, lambda e: (0,) * len(a.shape))

    if dist == 4:
        shapes = [(16 + half_rows, width), (half_rows, width)]
    elif dist == 0:
        shapes = [(EXPERTS, CAP + 16, width)]
    else:
        shapes = [(full, width), (full, width)]
    out_shape = [jax.ShapeDtypeStruct(s, BF) for s in shapes]
    if dist == 0:
        out_specs = [pl.BlockSpec((1, CAP + 16, width), lambda e: (e, 0, 0))]
    else:
        out_specs = [whole(s) for s in out_shape]
    return pl.pallas_call(
        functools.partial(backward_kernel, dist),
        grid=(EXPERTS,),
        in_specs=[whole(a) for a in (*small, *received)]
        + [pl.BlockSpec((1, width, hidden), lambda e: (0, e, 0))] * 2,
        out_specs=out_specs,
        out_shape=out_shape,
        compiler_params=pltpu.CompilerParams(vmem_limit_bytes=24 << 20),
        cost_estimate=pl.CostEstimate(
            flops=4 * 256 * EXPERTS * width * hidden,
            bytes_accessed=4 * EXPERTS * width * hidden,
            transcendentals=0,
        ),
        name="backward",
    )(*small, *received, w_gate, w_up)


def combine_kernel(ids_ref, weight_ref, rows_ref, out_ref):
    ind0, ind1, count = slot_masks(ids_ref[...])
    tokens = ind0.shape[1]
    width = rows_ref.shape[2]
    weights = weight_ref[...]
    scale = ind0 * weights[0:1, :] + ind1 * weights[1:2, :]
    slots = lax.broadcasted_iota(jnp.int32, (CAP, tokens), 0)
    total = jnp.zeros((tokens, width), F32)
    router0 = jnp.zeros((16, tokens), F32)
    router1 = jnp.zeros((16, tokens), F32)
    for e in range(EXPERTS):
        here = count[e : e + 1, :] == slots
        pick = jnp.where(here, scale[e : e + 1, :], 0.0)
        total += tn(pick, rows_ref[e, 0:CAP, :].astype(F32), precision=HIGH)
        slot_rows = rows_ref[e, CAP : CAP + 16, 0:128][:, :CAP].astype(F32)
        one0 = jnp.where(here, ind0[e : e + 1, :], 0.0)
        one1 = jnp.where(here, ind1[e : e + 1, :], 0.0)
        router0 += jnp.dot(slot_rows, one0, precision=HIGH, preferred_element_type=F32)
        router1 += jnp.dot(slot_rows, one1, precision=HIGH, preferred_element_type=F32)
    out_ref[0:tokens, :] = total.astype(BF)
    sum0 = router0[0:1] + router0[1:2]
    sum1 = router1[0:1] + router1[1:2]
    high0, high1 = sum0.astype(BF).astype(F32), sum1.astype(BF).astype(F32)
    row = lax.broadcasted_iota(jnp.int32, (16, tokens), 0)
    packed = jnp.where(row == 0, high0, 0.0) + jnp.where(row == 1, sum0 - high0, 0.0)
    packed = packed + jnp.where(row == 2, high1, 0.0) + jnp.where(row == 3, sum1 - high1, 0.0)
    out_ref[tokens : tokens + 16, :] = jnp.concatenate(
        [packed.astype(BF), jnp.zeros((16, width - tokens), BF)], axis=1
    )


def combine(ids, weights, rows):
    tokens = ids.shape[1]
    return pl.pallas_call(
        combine_kernel,
        out_shape=jax.ShapeDtypeStruct((tokens + 16, rows.shape[2]), BF),
        compiler_params=pltpu.CompilerParams(vmem_limit_bytes=24 << 20),
        name="combine",
    )(ids, weights, rows)


def finish_kernel(a_ref, b_ref, c_ref, d_ref, x_ref, r_ref):
    tokens = x_ref.shape[0]
    total = (a_ref[...].astype(F32) + c_ref[...].astype(F32)) + (
        b_ref[...].astype(F32) + d_ref[...].astype(F32)
    )
    x_ref[...] = total[:tokens].astype(BF)
    tail = total[tokens : tokens + 16, :tokens]
    r_ref[0:1, :] = tail[0:1] + tail[1:2]
    r_ref[1:2, :] = tail[2:3] + tail[3:4]


def finish(own, plus, two, minus):
    tokens = own.shape[0] - 16
    return pl.pallas_call(
        finish_kernel,
        out_shape=(
            jax.ShapeDtypeStruct((tokens, own.shape[1]), BF),
            jax.ShapeDtypeStruct((2, tokens), F32),
        ),
        compiler_params=pltpu.CompilerParams(vmem_limit_bytes=24 << 20),
        name="finish",
    )(own, plus, two, minus)


def shift(a, axis, by):
    n = lax.axis_size(axis)
    return lax.ppermute(a, axis, [(i, (i + by) % n) for i in range(n)])


def spread(stacked, split):
    plus, minus = shift(stacked, "tensor", 1), shift(stacked, "tensor", -1)
    ahead, behind = shift(plus[:split], "tensor", 1), shift(minus[split:], "tensor", -1)
    return stacked, plus, minus, ahead, behind


def per_device(tokens, out_grad, expert_ids, combine_weights, w_gate, w_up, w_down):
    ids = expert_ids.T
    weights = combine_weights.T
    half = EXPERTS // 2
    place = jnp.stack([lax.axis_index("dp"), lax.axis_index("tensor")]).astype(jnp.int32)
    send = dispatch(place, ids, tokens, out_grad)
    own = lax.all_to_all(send, "expert", split_axis=0, concat_axis=0)
    whole, part = own[:, :, : 2 * WHOLE], own[:, :, 2 * WHOLE :]

    up, down = part, part
    behind, ahead = {}, {}
    for dist in range(1, 4):
        up, down = shift(up, "dp", 1), shift(down, "dp", -1)
        behind[dist], ahead[dist] = up, down
    low, high = shift(up[:half], "dp", 1), shift(down[half:], "dp", -1)
    whole = lax.optimization_barrier((whole, behind[1], ahead[1]))[0]
    whole = lax.all_gather(whole, "dp", axis=0)

    near = [part] + [shift(part, "tensor", by) for by in (1, -1, 2)]
    stacked = jnp.concatenate([ahead[1], ahead[2], behind[1], behind[2]], axis=0)
    near += [a.reshape(-1, EXPERTS, *a.shape[1:]) for a in spread(stacked, 2 * EXPERTS)]
    stacked = jnp.concatenate([ahead[3], low, behind[3], high], axis=0)
    far = [a.reshape(-1, half, *a.shape[1:]) for a in spread(stacked, EXPERTS + half)]

    outs = forward(pieces_near, (0, 1, 2, -1, -2), place, whole, near, w_gate, w_up, w_down)
    outs += forward(pieces_far, (3, -3, 4), place, whole, far, w_gate, w_up, w_down)
    grads = {0: [outs[0]], 1: [outs[1], outs[3]], 2: [outs[2], outs[4]]}
    grads.update({3: [outs[5], outs[6]], 4: [outs[7]]})
    received = ()
    for dist in range(4, 0, -1):
        small = [a for pair in grads[dist] for a in pair]
        plus, minus = backward(dist, small, received, w_gate, w_up)
        received = (shift(plus, "dp", 1), shift(minus, "dp", -1))
    (rows,) = backward(0, list(grads[0][0]), received, w_gate, w_up)
    rows = lax.all_to_all(rows, "expert", split_axis=0, concat_axis=0)
    part = combine(ids, weights, rows)
    x_grad, router = finish(
        part, shift(part, "tensor", 1), shift(part, "tensor", 2), shift(part, "tensor", -1)
    )
    return x_grad, router.T


def solution(mesh):
    placed = (
        P("dp", "expert"),
        P("dp", "expert"),
        P("dp", None),
        P("dp", None),
        P("expert", None, ("dp", "tensor")),
        P("expert", None, ("dp", "tensor")),
        P("expert", ("dp", "tensor"), None),
    )
    return jax.shard_map(
        per_device,
        mesh=mesh,
        in_specs=placed,
        out_specs=(P("dp", "expert"), P("dp", None)),
        check_vma=False,
    )
```

```python
import functools

import jax
import jax.numpy as jnp
from jax import lax
from jax.experimental import pallas as pl
from jax.experimental.pallas import tpu as pltpu
from jax.sharding import PartitionSpec as P

EXPERTS = 8
CAP = 48
WHOLE = 256
PART = 128
AHEAD = 6
BF = jnp.bfloat16
F32 = jnp.float32
HIGH = lax.Precision.HIGHEST


def nt(a, b, **kw):
    return lax.dot_general(a, b, (((1,), (1,)), ((), ())), preferred_element_type=F32, **kw)


def tn(a, b, **kw):
    return lax.dot_general(a, b, (((0,), (0,)), ((), ())), preferred_element_type=F32, **kw)


def slot_masks(ids):
    tokens = ids.shape[1]
    experts = lax.broadcasted_iota(jnp.int32, (EXPERTS, tokens), 0)
    ind0 = (ids[0:1, :] == experts).astype(F32)
    ind1 = (ids[1:2, :] == experts).astype(F32)
    before = (
        lax.broadcasted_iota(jnp.int32, (tokens, tokens), 0)
        < lax.broadcasted_iota(jnp.int32, (tokens, tokens), 1)
    )
    count = jnp.dot((ind0 + ind1).astype(BF), before.astype(BF), preferred_element_type=F32)
    return ind0, ind1, count.astype(jnp.int32)


def dispatch_kernel(place_ref, ids_ref, tok_ref, og_ref, tok_out, og_out):
    ind0, ind1, count = slot_masks(ids_ref[...])
    ind = ind0 + ind1
    tokens = ind.shape[1]
    slots = lax.broadcasted_iota(jnp.int32, (CAP, tokens), 0)
    quarter = pl.ds(pl.multiple_of(WHOLE + place_ref[0] * PART, 128), PART)
    og = jnp.concatenate([og_ref[:, 0:WHOLE], og_ref[:, quarter]], axis=1)
    for e in range(EXPERTS):
        pick = jnp.where(count[e : e + 1, :] == slots, ind[e : e + 1, :], 0.0).astype(BF)
        tok_out[e] = jnp.dot(pick, tok_ref[...], preferred_element_type=F32).astype(BF)
        og_out[e] = jnp.dot(pick, og, preferred_element_type=F32).astype(BF)


def dispatch(place, ids, tokens, out_grad):
    width = tokens.shape[1]
    return pl.pallas_call(
        dispatch_kernel,
        in_specs=[pl.BlockSpec(memory_space=pltpu.SMEM)]
        + [pl.BlockSpec(memory_space=pltpu.VMEM)] * 3,
        out_shape=[
            jax.ShapeDtypeStruct((EXPERTS, CAP, width), BF),
            jax.ShapeDtypeStruct((EXPERTS, CAP, WHOLE + PART), BF),
        ],
        compiler_params=pltpu.CompilerParams(vmem_limit_bytes=24 << 20),
        name="dispatch",
    )(place, ids, tokens, out_grad)


def forward_kernel(count, split, n_after, place_ref, *refs):
    n_tok = 2 if split else count
    toks, ogs = refs[:n_tok], refs[n_tok : n_tok + count]
    refs = refs[n_tok + count :]
    quarters = [refs[3 * i : 3 * i + 3] for i in range(count)]
    refs = refs[3 * count + n_after :]
    wg_ref, wu_ref, wd_ref = refs[:3]
    outs = refs[3 : 3 + 2 * count]
    acc_g, acc_u, acc_b, og_ref = refs[3 + 2 * count :]
    e = pl.program_id(0)

    @pl.when(e == 0)
    def _():
        acc_g[...] = jnp.zeros_like(acc_g)
        acc_u[...] = jnp.zeros_like(acc_u)
        acc_b[...] = jnp.zeros_like(acc_b)

    for i in range(count):
        rows = slice(i * CAP, (i + 1) * CAP)
        og_ref[rows, 0:WHOLE] = ogs[i][0, :, 0:WHOLE]
        pieces = [ogs[i][0, :, WHOLE : WHOLE + PART], *[r[0, 0] for r in quarters[i]]]
        for piece, offset in zip(pieces, (0, 3, 1, 2)):
            there = lax.rem(place_ref[0] + offset, 4)
            og_ref[rows, pl.ds(pl.multiple_of(WHOLE + there * PART, 128), PART)] = piece
    if split:
        tok = jnp.where(e < AHEAD, toks[0][0], toks[1][0])
    else:
        tok = jnp.concatenate([r[0] for r in toks], axis=0)
    acc_g[...] += jnp.dot(tok, wg_ref[0], preferred_element_type=F32)
    acc_u[...] += jnp.dot(tok, wu_ref[0], preferred_element_type=F32)
    acc_b[...] += nt(og_ref[...], wd_ref[0])

    @pl.when(e == EXPERTS - 1)
    def _():
        gate, up, back = acc_g[...], acc_u[...], acc_b[...]
        sig = jax.nn.sigmoid(gate)
        act = gate * sig
        prod = back * (act * up)
        grad_up = (back * act).astype(BF)
        grad_gate = (back * up * sig * (1.0 + gate * (1.0 - sig))).astype(BF)
        hidden = gate.shape[1]
        ones = jnp.ones((16, hidden), F32)
        fill = jnp.zeros((128 - CAP, hidden), F32)
        for i in range(count):
            rows = slice(i * CAP, (i + 1) * CAP)
            outs[2 * i][:, :hidden] = grad_gate[rows]
            outs[2 * i][:, hidden:] = grad_up[rows]
            outs[2 * i + 1][...] = nt(
                ones, jnp.concatenate([prod[rows], fill], axis=0), precision=HIGH
            )


def forward(place, toks, ogs, quarters, after, w_gate, w_up, w_down):
    hidden = w_gate.shape[2]
    width = toks[0].shape[2]
    count = len(ogs)
    split = len(toks) > count
    if split:
        in_specs = [
            pl.BlockSpec((1, CAP, width), lambda e, at: (jnp.minimum(e, AHEAD - 1), 0, 0)),
            pl.BlockSpec((1, CAP, width), lambda e, at: (jnp.maximum(e - AHEAD, 0), 0, 0)),
        ]
    else:
        in_specs = [pl.BlockSpec((1, CAP, width), lambda e, at: (e, 0, 0))] * count
    in_specs += [pl.BlockSpec((1, CAP, WHOLE + PART), lambda e, at: (e, 0, 0))] * count
    operands = []

    def quarter_spec(index):
        return pl.BlockSpec((1, 1, CAP, PART), lambda e, at: (index, e, 0, 0))

    for index, arrays in quarters:
        in_specs += [quarter_spec(index)] * 3
        operands += arrays
    in_specs += [pl.BlockSpec(memory_space=pl.ANY)] * len(after)
    in_specs += [
        pl.BlockSpec((1, width, hidden), lambda e, at: (0, e, 0)),
        pl.BlockSpec((1, width, hidden), lambda e, at: (0, e, 0)),
        pl.BlockSpec((1, hidden, width), lambda e, at: (0, 0, e)),
    ]
    rows = count * CAP
    outs = pl.pallas_call(
        functools.partial(forward_kernel, count, split, len(after)),
        grid_spec=pltpu.PrefetchScalarGridSpec(
            num_scalar_prefetch=1,
            grid=(EXPERTS,),
            in_specs=in_specs,
            out_specs=[
                pl.BlockSpec((CAP, 2 * hidden), lambda e, at: (0, 0)),
                pl.BlockSpec((16, 128), lambda e, at: (0, 0)),
            ]
            * count,
            scratch_shapes=[pltpu.VMEM((rows, hidden), F32)] * 3 + [pltpu.VMEM((rows, width), BF)],
        ),
        out_shape=[
            jax.ShapeDtypeStruct((CAP, 2 * hidden), BF),
            jax.ShapeDtypeStruct((16, 128), F32),
        ]
        * count,
        compiler_params=pltpu.CompilerParams(vmem_limit_bytes=24 << 20),
        cost_estimate=pl.CostEstimate(
            flops=6 * 256 * EXPERTS * width * hidden,
            bytes_accessed=6 * EXPERTS * width * hidden,
            transcendentals=0,
        ),
        name="forward",
    )(place, *toks, *ogs, *operands, *after, w_gate, w_up, w_down)
    return [(outs[2 * i], outs[2 * i + 1]) for i in range(count)]


def pack_slots(total, width):
    high = total.astype(BF).astype(F32)
    low = total - high
    row = lax.broadcasted_iota(jnp.int32, (16, 128), 0)
    packed = jnp.where(row == 0, high, jnp.where(row == 1, low, 0.0)).astype(BF)
    return jnp.concatenate([packed, jnp.zeros((16, width - 128), BF)], axis=1)


def unpack_slots(rows):
    packed = rows.astype(F32)
    return packed[0:1] + packed[1:2]


def product(grads, wg_ref, wu_ref, e):
    hidden = wg_ref.shape[2]
    width = wg_ref.shape[1] // EXPERTS
    part = pl.ds(pl.multiple_of(e * width, width), width)
    return nt(grads[:, :hidden], wg_ref[0, part, :]) + nt(grads[:, hidden:], wu_ref[0, part, :])


def backward_kernel(ways, got, first, wg_ref, wu_ref, *refs):
    grads, slots, received, outs = (refs[i * ways : (i + 1) * ways] for i in range(4))
    if not got:
        outs = received
    skip = 0 if first else 16
    if not first:
        for i in range(ways):
            total = slots[i][0:1, :]
            if got:
                total = total + unpack_slots(received[i][0:16, 0:128])
            outs[i][0:16, :] = pack_slots(total, outs[i].shape[1])
    rows_of = jnp.concatenate([r[...] for r in grads], axis=0)

    @pl.loop(0, EXPERTS // 2)
    def _(e):
        part = product(rows_of, wg_ref, wu_ref, first + e)
        rows = pl.ds(pl.multiple_of(skip + e * CAP, 16), CAP)
        for i in range(ways):
            own = part[i * CAP : (i + 1) * CAP]
            if got:
                own = own + received[i][rows, :].astype(F32)
            outs[i][rows, :] = own.astype(BF)


def backward(first, small, received, w_gate, w_up):
    hidden = w_gate.shape[2]
    width = w_gate.shape[1] // EXPERTS
    ways = len(small)
    rows = CAP * EXPERTS // 2 + (0 if first else 16)
    operands = [w_gate, w_up, *[a for a, _ in small], *[a for _, a in small], *received]
    return pl.pallas_call(
        functools.partial(backward_kernel, ways, bool(received), first),
        in_specs=[pl.BlockSpec(memory_space=pltpu.VMEM)] * len(operands),
        out_shape=[jax.ShapeDtypeStruct((rows, width), BF)] * ways,
        compiler_params=pltpu.CompilerParams(vmem_limit_bytes=24 << 20),
        cost_estimate=pl.CostEstimate(
            flops=2 * 256 * EXPERTS * width * hidden,
            bytes_accessed=2 * EXPERTS * width * hidden,
            transcendentals=0,
        ),
        name="backward",
    )(*operands)


def last_kernel(g_ref, s_ref, *refs):
    low, high = refs[0:2], refs[2:4]
    wg_ref, wu_ref, out_ref = refs[4:]
    half = EXPERTS // 2
    grads = g_ref[...]
    total = s_ref[0:1, :] + (unpack_slots(low[0][0:16, 0:128]) + unpack_slots(low[1][0:16, 0:128]))
    tail = pack_slots(total, out_ref.shape[2])
    for first, skip, parts in ((0, 16, low), (half, 0, high)):

        @pl.loop(0, half)
        def _(e):
            rows = pl.ds(pl.multiple_of(skip + e * CAP, 16), CAP)
            sums = parts[0][rows, :].astype(F32) + parts[1][rows, :].astype(F32)
            own = product(grads, wg_ref, wu_ref, first + e)
            out_ref[first + e, 0:CAP, :] = (own + sums).astype(BF)
            out_ref[first + e, CAP : CAP + 16, :] = tail


def last(small, low, high, w_gate, w_up):
    operands = [*small, *low, *high, w_gate, w_up]
    return pl.pallas_call(
        last_kernel,
        in_specs=[pl.BlockSpec(memory_space=pltpu.VMEM)] * len(operands),
        out_shape=jax.ShapeDtypeStruct((EXPERTS, CAP + 16, high[0].shape[1]), BF),
        compiler_params=pltpu.CompilerParams(vmem_limit_bytes=24 << 20),
        name="last",
    )(*operands)


def combine_kernel(ids_ref, weight_ref, rows_ref, out_ref):
    ind0, ind1, count = slot_masks(ids_ref[...])
    tokens = ind0.shape[1]
    width = rows_ref.shape[2]
    weights = weight_ref[...]
    scale = ind0 * weights[0:1, :] + ind1 * weights[1:2, :]
    slots = lax.broadcasted_iota(jnp.int32, (CAP, tokens), 0)
    total = jnp.zeros((tokens, width), F32)
    router0 = jnp.zeros((16, tokens), F32)
    router1 = jnp.zeros((16, tokens), F32)
    for e in range(EXPERTS):
        here = count[e : e + 1, :] == slots
        pick = jnp.where(here, scale[e : e + 1, :], 0.0)
        total += tn(pick, rows_ref[e, 0:CAP, :].astype(F32), precision=HIGH)
        slot_rows = rows_ref[e, CAP : CAP + 16, 0:128][:, :CAP].astype(F32)
        one0 = jnp.where(here, ind0[e : e + 1, :], 0.0)
        one1 = jnp.where(here, ind1[e : e + 1, :], 0.0)
        router0 += jnp.dot(slot_rows, one0, precision=HIGH, preferred_element_type=F32)
        router1 += jnp.dot(slot_rows, one1, precision=HIGH, preferred_element_type=F32)
    out_ref[0:tokens, :] = total.astype(BF)
    sum0 = router0[0:1] + router0[1:2]
    sum1 = router1[0:1] + router1[1:2]
    high0, high1 = sum0.astype(BF).astype(F32), sum1.astype(BF).astype(F32)
    row = lax.broadcasted_iota(jnp.int32, (16, tokens), 0)
    packed = jnp.where(row == 0, high0, 0.0) + jnp.where(row == 1, sum0 - high0, 0.0)
    packed = packed + jnp.where(row == 2, high1, 0.0) + jnp.where(row == 3, sum1 - high1, 0.0)
    out_ref[tokens : tokens + 16, :] = jnp.concatenate(
        [packed.astype(BF), jnp.zeros((16, width - tokens), BF)], axis=1
    )


def combine(ids, weights, rows):
    tokens = ids.shape[1]
    return pl.pallas_call(
        combine_kernel,
        out_shape=jax.ShapeDtypeStruct((tokens + 16, rows.shape[2]), BF),
        compiler_params=pltpu.CompilerParams(vmem_limit_bytes=24 << 20),
        name="combine",
    )(ids, weights, rows)


def finish_kernel(a_ref, b_ref, c_ref, d_ref, x_ref, r_ref):
    tokens = x_ref.shape[0]
    total = (a_ref[...].astype(F32) + c_ref[...].astype(F32)) + (
        b_ref[...].astype(F32) + d_ref[...].astype(F32)
    )
    x_ref[...] = total[:tokens].astype(BF)
    tail = total[tokens : tokens + 16, :tokens]
    r_ref[0:1, :] = tail[0:1] + tail[1:2]
    r_ref[1:2, :] = tail[2:3] + tail[3:4]


def finish(own, plus, two, minus):
    tokens = own.shape[0] - 16
    return pl.pallas_call(
        finish_kernel,
        out_shape=(
            jax.ShapeDtypeStruct((tokens, own.shape[1]), BF),
            jax.ShapeDtypeStruct((2, tokens), F32),
        ),
        compiler_params=pltpu.CompilerParams(vmem_limit_bytes=24 << 20),
        name="finish",
    )(own, plus, two, minus)


def shift(a, axis, by):
    n = lax.axis_size(axis)
    return lax.ppermute(a, axis, [(i, (i + by) % n) for i in range(n)])


def per_device(tokens, out_grad, expert_ids, combine_weights, w_gate, w_up, w_down):
    ids = expert_ids.T
    weights = combine_weights.T
    half = EXPERTS // 2
    place = lax.axis_index("tensor").astype(jnp.int32)[None]
    tok, og = dispatch(place, ids, tokens, out_grad)
    og = lax.all_to_all(og, "expert", split_axis=0, concat_axis=0)
    tok = lax.all_to_all(tok, "expert", split_axis=0, concat_axis=0)

    toks, ogs = {0: tok}, {0: og}
    for dist in range(1, 4):
        for blocks in (ogs, toks):
            blocks[-dist] = shift(blocks[1 - dist], "dp", 1)
            blocks[dist] = shift(blocks[dist - 1], "dp", -1)
    ogs[4] = shift(ogs[3], "dp", -1)

    grads, after = {}, []
    for dists in ((0, 1, -1), (2, -2, 3, -3), (4,)):
        mine = jnp.concatenate([ogs[d][:, :, WHOLE:] for d in dists], axis=0)
        others = [shift(mine, "tensor", by) for by in (1, -1, 2)]
        others = [a.reshape(len(dists), EXPERTS, CAP, PART) for a in others]
        if dists == (4,):
            parts = lax.optimization_barrier((toks[-3][:AHEAD], toks[3][AHEAD:], after[0]))
            blocks = [shift(parts[0], "dp", 1), shift(parts[1], "dp", -1)]
        else:
            blocks = [toks[d] for d in dists]
        found = forward(
            place,
            blocks,
            [ogs[d] for d in dists],
            [(i, others) for i in range(len(dists))],
            after if dists == (4,) else [],
            w_gate,
            w_up,
            w_down,
        )
        grads.update(zip(dists, found))
        after.append(found[0][1])

    got = {0: (), half: ()}
    final = {0: {}, half: {}}
    for step in range(4):
        for first in (0, half):
            long = 1 if first == 0 else -1
            dists = [long * (4 - step)] + ([-long * (3 - step)] if step < 3 else [])
            small = [grads[4 if d == -4 else d] for d in dists]
            received = got[first][: len(dists)]
            outs = backward(first, small, received, w_gate, w_up)
            sent = [shift(o, "dp", 1 if d > 0 else -1) for o, d in zip(outs, dists)]
            got[first] = sent
            final[first].update({i: a for i, a in enumerate(sent)})
    low = [final[0][0], final[0][1]]
    high = [final[half][0], final[half][1]]
    rows = last(grads[0], low, high, w_gate, w_up)
    rows = lax.all_to_all(rows, "expert", split_axis=0, concat_axis=0)
    part = combine(ids, weights, rows)
    x_grad, router = finish(
        part, shift(part, "tensor", 1), shift(part, "tensor", 2), shift(part, "tensor", -1)
    )
    return x_grad, router.T


def solution(mesh):
    placed = (
        P("dp", "expert"),
        P("dp", "expert"),
        P("dp", None),
        P("dp", None),
        P("expert", None, ("dp", "tensor")),
        P("expert", None, ("dp", "tensor")),
        P("expert", ("dp", "tensor"), None),
    )
    return jax.shard_map(
        per_device,
        mesh=mesh,
        in_specs=placed,
        out_specs=(P("dp", "expert"), P("dp", None)),
        check_vma=False,
    )
```

```python
import functools

import jax
import jax.numpy as jnp
from jax import lax
from jax.experimental import pallas as pl
from jax.experimental.pallas import tpu as pltpu
from jax.sharding import PartitionSpec as P

EXPERTS = 8
CAP = 48
WHOLE = 256
PART = 128
AHEAD = 4
BF = jnp.bfloat16
F32 = jnp.float32
HIGH = lax.Precision.HIGHEST


def nt(a, b, **kw):
    return lax.dot_general(a, b, (((1,), (1,)), ((), ())), preferred_element_type=F32, **kw)


def tn(a, b, **kw):
    return lax.dot_general(a, b, (((0,), (0,)), ((), ())), preferred_element_type=F32, **kw)


def slot_masks(ids):
    tokens = ids.shape[1]
    experts = lax.broadcasted_iota(jnp.int32, (EXPERTS, tokens), 0)
    ind0 = (ids[0:1, :] == experts).astype(F32)
    ind1 = (ids[1:2, :] == experts).astype(F32)
    before = (
        lax.broadcasted_iota(jnp.int32, (tokens, tokens), 0)
        < lax.broadcasted_iota(jnp.int32, (tokens, tokens), 1)
    )
    count = jnp.dot((ind0 + ind1).astype(BF), before.astype(BF), preferred_element_type=F32)
    return ind0, ind1, count.astype(jnp.int32)


def dispatch_kernel(place_ref, ids_ref, tok_ref, og_ref, out_ref):
    ind0, ind1, count = slot_masks(ids_ref[...])
    ind = ind0 + ind1
    tokens = ind.shape[1]
    slots = lax.broadcasted_iota(jnp.int32, (CAP, tokens), 0)
    quarter = pl.ds(pl.multiple_of(WHOLE + place_ref[0] * PART, 128), PART)
    og = jnp.concatenate([og_ref[:, 0:WHOLE], og_ref[:, quarter]], axis=1)
    for e in range(EXPERTS):
        pick = jnp.where(count[e : e + 1, :] == slots, ind[e : e + 1, :], 0.0).astype(BF)
        width = tok_ref.shape[1]
        out_ref[e, :, :width] = jnp.dot(
            pick, tok_ref[...], preferred_element_type=F32
        ).astype(BF)
        out_ref[e, :, width:] = jnp.dot(pick, og, preferred_element_type=F32).astype(BF)


def dispatch(place, ids, tokens, out_grad):
    width = tokens.shape[1]
    return pl.pallas_call(
        dispatch_kernel,
        in_specs=[pl.BlockSpec(memory_space=pltpu.SMEM)]
        + [pl.BlockSpec(memory_space=pltpu.VMEM)] * 3,
        out_shape=jax.ShapeDtypeStruct((EXPERTS, CAP, width + WHOLE + PART), BF),
        compiler_params=pltpu.CompilerParams(vmem_limit_bytes=24 << 20),
        name="dispatch",
    )(place, ids, tokens, out_grad)


def forward_kernel(count, split, n_after, place_ref, *refs):
    toks, ogs = refs[: count + split], refs[count + split : 2 * (count + split)]
    refs = refs[2 * (count + split) :]
    owns = refs[:count]
    quarters = [refs[count + 3 * i : count + 3 * i + 3] for i in range(count)]
    refs = refs[4 * count + n_after :]
    wg_ref, wu_ref, wd_ref = refs[:3]
    outs = refs[3 : 3 + 2 * count]
    acc_g, acc_u, acc_b, og_ref = refs[3 + 2 * count :]
    e = pl.program_id(0)

    @pl.when(e == 0)
    def _():
        acc_g[...] = jnp.zeros_like(acc_g)
        acc_u[...] = jnp.zeros_like(acc_u)
        acc_b[...] = jnp.zeros_like(acc_b)

    tok, og = [r[0] for r in toks[:count]], [r[0] for r in ogs[:count]]
    if split:
        tok[-1] = jnp.where(e < AHEAD, tok[-1], toks[count][0])
        og[-1] = jnp.where(e < AHEAD, og[-1], ogs[count][0])
    tok = jnp.concatenate(tok, axis=0)
    for i in range(count):
        rows = slice(i * CAP, (i + 1) * CAP)
        og_ref[rows, 0:WHOLE] = og[i]
        pieces = [owns[i][0], *[r[0, 0] for r in quarters[i]]]
        for piece, offset in zip(pieces, (0, 3, 1, 2)):
            there = lax.rem(place_ref[0] + offset, 4)
            og_ref[rows, pl.ds(pl.multiple_of(WHOLE + there * PART, 128), PART)] = piece
    acc_g[...] += jnp.dot(tok, wg_ref[0], preferred_element_type=F32)
    acc_u[...] += jnp.dot(tok, wu_ref[0], preferred_element_type=F32)
    acc_b[...] += nt(og_ref[...], wd_ref[0])

    @pl.when(e == EXPERTS - 1)
    def _():
        gate, up, back = acc_g[...], acc_u[...], acc_b[...]
        sig = jax.nn.sigmoid(gate)
        act = gate * sig
        prod = back * (act * up)
        grad_up = (back * act).astype(BF)
        grad_gate = (back * up * sig * (1.0 + gate * (1.0 - sig))).astype(BF)
        hidden = gate.shape[1]
        ones = jnp.ones((16, hidden), F32)
        fill = jnp.zeros((128 - CAP, hidden), F32)
        for i in range(count):
            rows = slice(i * CAP, (i + 1) * CAP)
            outs[2 * i][:, :hidden] = grad_gate[rows]
            outs[2 * i][:, hidden:] = grad_up[rows]
            outs[2 * i + 1][...] = nt(
                ones, jnp.concatenate([prod[rows], fill], axis=0), precision=HIGH
            )


def forward(place, blocks, owns, quarters, after, w_gate, w_up, w_down):
    hidden = w_gate.shape[2]
    width = w_gate.shape[1] // EXPERTS
    count = len(quarters)
    split = len(blocks) - count
    slices = [lambda e: e] * count
    if split:
        slices[-1:] = [
            lambda e: jnp.minimum(e, AHEAD - 1),
            lambda e: jnp.maximum(e - AHEAD, 0),
        ]

    def tok_spec(at):
        return pl.BlockSpec((1, CAP, width), lambda e, _: (at(e), 0, 0))

    def og_spec(at):
        return pl.BlockSpec((1, CAP, WHOLE), lambda e, _: (at(e), 0, width // WHOLE))

    def own_spec(column):
        return pl.BlockSpec((1, CAP, PART), lambda e, _: (e, 0, column))

    in_specs = [tok_spec(at) for at in slices] + [og_spec(at) for at in slices]
    in_specs += [own_spec(a.shape[2] // PART - 1) for a in owns]
    operands = []

    def quarter_spec(index):
        return pl.BlockSpec((1, 1, CAP, PART), lambda e, at: (index, e, 0, 0))

    for index, arrays in quarters:
        in_specs += [quarter_spec(index)] * 3
        operands += arrays
    in_specs += [pl.BlockSpec(memory_space=pl.ANY)] * len(after)
    in_specs += [
        pl.BlockSpec((1, width, hidden), lambda e, at: (0, e, 0)),
        pl.BlockSpec((1, width, hidden), lambda e, at: (0, e, 0)),
        pl.BlockSpec((1, hidden, width), lambda e, at: (0, 0, e)),
    ]
    rows = count * CAP
    outs = pl.pallas_call(
        functools.partial(forward_kernel, count, split, len(after)),
        grid_spec=pltpu.PrefetchScalarGridSpec(
            num_scalar_prefetch=1,
            grid=(EXPERTS,),
            in_specs=in_specs,
            out_specs=[
                pl.BlockSpec((CAP, 2 * hidden), lambda e, at: (0, 0)),
                pl.BlockSpec((16, 128), lambda e, at: (0, 0)),
            ]
            * count,
            scratch_shapes=[pltpu.VMEM((rows, hidden), F32)] * 3 + [pltpu.VMEM((rows, width), BF)],
        ),
        out_shape=[
            jax.ShapeDtypeStruct((CAP, 2 * hidden), BF),
            jax.ShapeDtypeStruct((16, 128), F32),
        ]
        * count,
        compiler_params=pltpu.CompilerParams(vmem_limit_bytes=24 << 20),
        cost_estimate=pl.CostEstimate(
            flops=6 * 256 * EXPERTS * width * hidden,
            bytes_accessed=6 * EXPERTS * width * hidden,
            transcendentals=0,
        ),
        name="forward",
    )(place, *blocks, *blocks, *owns, *operands, *after, w_gate, w_up, w_down)
    return [(outs[2 * i], outs[2 * i + 1]) for i in range(count)]


def pack_slots(total, width):
    high = total.astype(BF).astype(F32)
    low = total - high
    row = lax.broadcasted_iota(jnp.int32, (16, 128), 0)
    packed = jnp.where(row == 0, high, jnp.where(row == 1, low, 0.0)).astype(BF)
    return jnp.concatenate([packed, jnp.zeros((16, width - 128), BF)], axis=1)


def unpack_slots(rows):
    packed = rows.astype(F32)
    return packed[0:1] + packed[1:2]


def product(grads, wg_ref, wu_ref, e):
    hidden = wg_ref.shape[2]
    width = wg_ref.shape[1] // EXPERTS
    part = pl.ds(pl.multiple_of(e * width, width), width)
    return nt(grads[:, :hidden], wg_ref[0, part, :]) + nt(grads[:, hidden:], wu_ref[0, part, :])


def backward_kernel(ways, got, first, wg_ref, wu_ref, *refs):
    grads, slots, received, outs = (refs[i * ways : (i + 1) * ways] for i in range(4))
    if not got:
        outs = received
    skip = 0 if first else 16
    if not first:
        for i in range(ways):
            total = slots[i][0:1, :]
            if got:
                total = total + unpack_slots(received[i][0:16, 0:128])
            outs[i][0:16, :] = pack_slots(total, outs[i].shape[1])
    rows_of = jnp.concatenate([r[...] for r in grads], axis=0)

    @pl.loop(0, EXPERTS // 2)
    def _(e):
        part = product(rows_of, wg_ref, wu_ref, first + e)
        rows = pl.ds(pl.multiple_of(skip + e * CAP, 16), CAP)
        for i in range(ways):
            own = part[i * CAP : (i + 1) * CAP]
            if got:
                own = own + received[i][rows, :].astype(F32)
            outs[i][rows, :] = own.astype(BF)


def backward(first, small, received, w_gate, w_up):
    hidden = w_gate.shape[2]
    width = w_gate.shape[1] // EXPERTS
    ways = len(small)
    rows = CAP * EXPERTS // 2 + (0 if first else 16)
    operands = [w_gate, w_up, *[a for a, _ in small], *[a for _, a in small], *received]
    return pl.pallas_call(
        functools.partial(backward_kernel, ways, bool(received), first),
        in_specs=[pl.BlockSpec(memory_space=pltpu.VMEM)] * len(operands),
        out_shape=[jax.ShapeDtypeStruct((rows, width), BF)] * ways,
        compiler_params=pltpu.CompilerParams(vmem_limit_bytes=24 << 20),
        cost_estimate=pl.CostEstimate(
            flops=2 * 256 * EXPERTS * width * hidden,
            bytes_accessed=2 * EXPERTS * width * hidden,
            transcendentals=0,
        ),
        name="backward",
    )(*operands)


def own_kernel(g_ref, wg_ref, wu_ref, out_ref):
    grads = g_ref[...]

    @pl.loop(0, EXPERTS)
    def _(e):
        out_ref[e] = product(grads, wg_ref, wu_ref, e)


def own_product(grads, w_gate, w_up):
    hidden = w_gate.shape[2]
    width = w_gate.shape[1] // EXPERTS
    return pl.pallas_call(
        own_kernel,
        in_specs=[pl.BlockSpec(memory_space=pltpu.VMEM)] * 3,
        out_shape=jax.ShapeDtypeStruct((EXPERTS, CAP, width), F32),
        compiler_params=pltpu.CompilerParams(vmem_limit_bytes=24 << 20),
        cost_estimate=pl.CostEstimate(
            flops=2 * 256 * EXPERTS * width * hidden,
            bytes_accessed=4 * EXPERTS * width * hidden,
            transcendentals=0,
        ),
        name="own_product",
    )(grads, w_gate, w_up)


def last_kernel(own_ref, s_ref, *refs):
    low, high, out_ref = refs[0:2], refs[2:4], refs[4]
    half = EXPERTS // 2
    total = s_ref[0:1, :] + (unpack_slots(low[0][0:16, 0:128]) + unpack_slots(low[1][0:16, 0:128]))
    tail = pack_slots(total, out_ref.shape[2])
    for e in range(EXPERTS):
        parts, start = (low, 16 + e * CAP) if e < half else (high, (e - half) * CAP)
        rows = slice(start, start + CAP)
        sums = parts[0][rows, :].astype(F32) + parts[1][rows, :].astype(F32)
        out_ref[e, 0:CAP, :] = (own_ref[e] + sums).astype(BF)
        out_ref[e, CAP : CAP + 16, :] = tail


def last(own, slots, low, high):
    operands = [own, slots, *low, *high]
    return pl.pallas_call(
        last_kernel,
        in_specs=[pl.BlockSpec(memory_space=pltpu.VMEM)] * len(operands),
        out_shape=jax.ShapeDtypeStruct((EXPERTS, CAP + 16, own.shape[2]), BF),
        compiler_params=pltpu.CompilerParams(vmem_limit_bytes=24 << 20),
        name="last",
    )(*operands)


def combine_kernel(ids_ref, weight_ref, rows_ref, out_ref):
    ind0, ind1, count = slot_masks(ids_ref[...])
    tokens = ind0.shape[1]
    width = rows_ref.shape[2]
    weights = weight_ref[...]
    scale = ind0 * weights[0:1, :] + ind1 * weights[1:2, :]
    slots = lax.broadcasted_iota(jnp.int32, (CAP, tokens), 0)
    picks = []
    router0 = jnp.zeros((16, tokens), F32)
    router1 = jnp.zeros((16, tokens), F32)
    for e in range(EXPERTS):
        here = count[e : e + 1, :] == slots
        picks.append(jnp.where(here, scale[e : e + 1, :], 0.0))
        slot_rows = rows_ref[e, CAP : CAP + 16, 0:128][:, :CAP]
        one0 = jnp.where(here, ind0[e : e + 1, :], 0.0).astype(BF)
        one1 = jnp.where(here, ind1[e : e + 1, :], 0.0).astype(BF)
        router0 += jnp.dot(slot_rows, one0, preferred_element_type=F32)
        router1 += jnp.dot(slot_rows, one1, preferred_element_type=F32)
    rest = jnp.concatenate(picks, axis=0)
    rows = jnp.concatenate([rows_ref[e, 0:CAP, :] for e in range(EXPERTS)], axis=0)
    total = jnp.zeros((tokens, width), F32)
    for _ in range(3):
        part = rest.astype(BF)
        total += tn(part, rows)
        rest = rest - part.astype(F32)
    out_ref[0:tokens, :] = total.astype(BF)
    sum0 = router0[0:1] + router0[1:2]
    sum1 = router1[0:1] + router1[1:2]
    high0, high1 = sum0.astype(BF).astype(F32), sum1.astype(BF).astype(F32)
    row = lax.broadcasted_iota(jnp.int32, (16, tokens), 0)
    packed = jnp.where(row == 0, high0, 0.0) + jnp.where(row == 1, sum0 - high0, 0.0)
    packed = packed + jnp.where(row == 2, high1, 0.0) + jnp.where(row == 3, sum1 - high1, 0.0)
    out_ref[tokens : tokens + 16, :] = jnp.concatenate(
        [packed.astype(BF), jnp.zeros((16, width - tokens), BF)], axis=1
    )


def combine(ids, weights, rows):
    tokens = ids.shape[1]
    return pl.pallas_call(
        combine_kernel,
        out_shape=jax.ShapeDtypeStruct((tokens + 16, rows.shape[2]), BF),
        compiler_params=pltpu.CompilerParams(vmem_limit_bytes=24 << 20),
        name="combine",
    )(ids, weights, rows)


def finish_kernel(a_ref, b_ref, c_ref, d_ref, x_ref, r_ref):
    tokens = x_ref.shape[0]
    total = (a_ref[...].astype(F32) + c_ref[...].astype(F32)) + (
        b_ref[...].astype(F32) + d_ref[...].astype(F32)
    )
    x_ref[...] = total[:tokens].astype(BF)
    tail = total[tokens : tokens + 16, :tokens]
    r_ref[0:1, :] = tail[0:1] + tail[1:2]
    r_ref[1:2, :] = tail[2:3] + tail[3:4]


def finish(own, plus, two, minus):
    tokens = own.shape[0] - 16
    return pl.pallas_call(
        finish_kernel,
        out_shape=(
            jax.ShapeDtypeStruct((tokens, own.shape[1]), BF),
            jax.ShapeDtypeStruct((2, tokens), F32),
        ),
        compiler_params=pltpu.CompilerParams(vmem_limit_bytes=24 << 20),
        name="finish",
    )(own, plus, two, minus)


def shift(a, axis, by):
    n = lax.axis_size(axis)
    return lax.ppermute(a, axis, [(i, (i + by) % n) for i in range(n)])


def per_device(tokens, out_grad, expert_ids, combine_weights, w_gate, w_up, w_down):
    ids = expert_ids.T
    weights = combine_weights.T
    half = EXPERTS // 2
    place = lax.axis_index("tensor").astype(jnp.int32)[None]
    own = dispatch(place, ids, tokens, out_grad)
    own = lax.all_to_all(own, "expert", split_axis=0, concat_axis=0)

    width = own.shape[2] - PART
    blocks = {0: own}
    owns = {4: shift(own[:, :, width:], "dp", 4)}
    quarters = {}

    def spread(*dists):
        mine = jnp.concatenate([owns[d][:, :, -PART:] for d in dists], axis=0)
        others = [shift(mine, "tensor", by) for by in (1, -1, 2)]
        shaped = [a.reshape(len(dists), EXPERTS, CAP, PART) for a in others]
        quarters.update({d: (i, shaped) for i, d in enumerate(dists)})
        return others

    def hop(dist, beside):
        ahead, behind, *_ = lax.optimization_barrier((blocks[dist - 1], blocks[1 - dist], *beside))
        owns[dist] = blocks[dist] = shift(ahead, "dp", -1)
        owns[-dist] = blocks[-dist] = shift(behind, "dp", 1)

    owns[0] = own
    hop(1, [])
    hop(2, [owns[4]])
    hop(3, spread(0, 4))
    beside = spread(1, -1, 2, -2)
    low, high, *_ = lax.optimization_barrier(
        (blocks[-3][:AHEAD, :, :width], blocks[3][AHEAD:, :, :width], *beside)
    )
    split = [shift(low, "dp", 1), shift(high, "dp", -1)]
    spread(3, -3)

    grads = {}
    for dists in ((0, 1, -1, 2, -2), (3, -3, 4)):
        arrays = [blocks[d] for d in dists if d != 4] + (split if 4 in dists else [])
        found = forward(
            place,
            arrays,
            [owns[d] for d in dists],
            [quarters[d] for d in dists],
            [a for _, a in grads.values()][:1],
            w_gate,
            w_up,
            w_down,
        )
        grads.update(zip(dists, found))

    got = {0: (), half: ()}
    final = {0: {}, half: {}}
    for step in range(4):
        for first in (0, half):
            long = 1 if first == 0 else -1
            dists = [long * (4 - step)] + ([-long * (3 - step)] if step < 3 else [])
            small = [grads[4 if d == -4 else d] for d in dists]
            received = got[first][: len(dists)]
            outs = backward(first, small, received, w_gate, w_up)
            sent = [shift(o, "dp", 1 if d > 0 else -1) for o, d in zip(outs, dists)]
            got[first] = sent
            final[first].update({i: a for i, a in enumerate(sent)})
    low = [final[0][0], final[0][1]]
    high = [final[half][0], final[half][1]]
    rows = last(own_product(grads[0][0], w_gate, w_up), grads[0][1], low, high)
    rows = lax.all_to_all(rows, "expert", split_axis=0, concat_axis=0)
    part = combine(ids, weights, rows)
    x_grad, router = finish(
        part, shift(part, "tensor", 1), shift(part, "tensor", 2), shift(part, "tensor", -1)
    )
    return x_grad, router.T


def solution(mesh):
    placed = (
        P("dp", "expert"),
        P("dp", "expert"),
        P("dp", None),
        P("dp", None),
        P("expert", None, ("dp", "tensor")),
        P("expert", None, ("dp", "tensor")),
        P("expert", ("dp", "tensor"), None),
    )
    return jax.shard_map(
        per_device,
        mesh=mesh,
        in_specs=placed,
        out_specs=(P("dp", "expert"), P("dp", None)),
        check_vma=False,
    )
```

```python
import functools

import jax
import jax.numpy as jnp
from jax import lax
from jax.experimental import pallas as pl
from jax.experimental.pallas import tpu as pltpu
from jax.sharding import PartitionSpec as P

EXPERTS = 8
CAP = 48
WHOLE = 256
PART = 128
AHEAD = 4
BF = jnp.bfloat16
F32 = jnp.float32
HIGH = lax.Precision.HIGHEST


def nt(a, b, **kw):
    return lax.dot_general(a, b, (((1,), (1,)), ((), ())), preferred_element_type=F32, **kw)


def tn(a, b, **kw):
    return lax.dot_general(a, b, (((0,), (0,)), ((), ())), preferred_element_type=F32, **kw)


def slot_masks(ids):
    tokens = ids.shape[1]
    experts = lax.broadcasted_iota(jnp.int32, (EXPERTS, tokens), 0)
    ind0 = (ids[0:1, :] == experts).astype(F32)
    ind1 = (ids[1:2, :] == experts).astype(F32)
    before = (
        lax.broadcasted_iota(jnp.int32, (tokens, tokens), 0)
        < lax.broadcasted_iota(jnp.int32, (tokens, tokens), 1)
    )
    count = jnp.dot((ind0 + ind1).astype(BF), before.astype(BF), preferred_element_type=F32)
    return ind0, ind1, count.astype(jnp.int32)


def dispatch_kernel(place_ref, ids_ref, tok_ref, og_ref, out_ref):
    ind0, ind1, count = slot_masks(ids_ref[...])
    ind = ind0 + ind1
    tokens = ind.shape[1]
    slots = lax.broadcasted_iota(jnp.int32, (CAP, tokens), 0)
    quarter = pl.ds(pl.multiple_of(WHOLE + place_ref[0] * PART, 128), PART)
    og = jnp.concatenate([og_ref[:, 0:WHOLE], og_ref[:, quarter]], axis=1)
    for e in range(EXPERTS):
        pick = jnp.where(count[e : e + 1, :] == slots, ind[e : e + 1, :], 0.0).astype(BF)
        width = tok_ref.shape[1]
        out_ref[e, :, :width] = jnp.dot(
            pick, tok_ref[...], preferred_element_type=F32
        ).astype(BF)
        out_ref[e, :, width:] = jnp.dot(pick, og, preferred_element_type=F32).astype(BF)


def dispatch(place, ids, tokens, out_grad):
    width = tokens.shape[1]
    return pl.pallas_call(
        dispatch_kernel,
        in_specs=[pl.BlockSpec(memory_space=pltpu.SMEM)]
        + [pl.BlockSpec(memory_space=pltpu.VMEM)] * 3,
        out_shape=jax.ShapeDtypeStruct((EXPERTS, CAP, width + WHOLE + PART), BF),
        compiler_params=pltpu.CompilerParams(vmem_limit_bytes=24 << 20),
        name="dispatch",
    )(place, ids, tokens, out_grad)


def forward_kernel(count, split, n_after, place_ref, *refs):
    toks, ogs = refs[: count + split], refs[count + split : 2 * (count + split)]
    refs = refs[2 * (count + split) :]
    owns = refs[:count]
    quarters = [refs[count + 3 * i : count + 3 * i + 3] for i in range(count)]
    refs = refs[4 * count + n_after :]
    wg_ref, wu_ref, wd_ref = refs[:3]
    outs = refs[3 : 3 + 2 * count]
    acc_g, acc_u, acc_b, og_ref = refs[3 + 2 * count :]
    e = pl.program_id(0)

    @pl.when(e == 0)
    def _():
        acc_g[...] = jnp.zeros_like(acc_g)
        acc_u[...] = jnp.zeros_like(acc_u)
        acc_b[...] = jnp.zeros_like(acc_b)

    tok, og = [r[0] for r in toks[:count]], [r[0] for r in ogs[:count]]
    if split:
        tok[-1] = jnp.where(e < AHEAD, tok[-1], toks[count][0])
        og[-1] = jnp.where(e < AHEAD, og[-1], ogs[count][0])
    tok = jnp.concatenate(tok, axis=0)
    for i in range(count):
        rows = slice(i * CAP, (i + 1) * CAP)
        og_ref[rows, 0:WHOLE] = og[i]
        pieces = [owns[i][0], *[r[0, 0] for r in quarters[i]]]
        for piece, offset in zip(pieces, (0, 3, 1, 2)):
            there = lax.rem(place_ref[0] + offset, 4)
            og_ref[rows, pl.ds(pl.multiple_of(WHOLE + there * PART, 128), PART)] = piece
    acc_g[...] += jnp.dot(tok, wg_ref[0], preferred_element_type=F32)
    acc_u[...] += jnp.dot(tok, wu_ref[0], preferred_element_type=F32)
    acc_b[...] += nt(og_ref[...], wd_ref[0])

    @pl.when(e == EXPERTS - 1)
    def _():
        gate, up, back = acc_g[...], acc_u[...], acc_b[...]
        sig = jax.nn.sigmoid(gate)
        act = gate * sig
        prod = back * (act * up)
        grad_up = (back * act).astype(BF)
        grad_gate = (back * up * sig * (1.0 + gate * (1.0 - sig))).astype(BF)
        hidden = gate.shape[1]
        ones = jnp.ones((16, hidden), F32)
        fill = jnp.zeros((128 - CAP, hidden), F32)
        for i in range(count):
            rows = slice(i * CAP, (i + 1) * CAP)
            outs[2 * i][:, :hidden] = grad_gate[rows]
            outs[2 * i][:, hidden:] = grad_up[rows]
            outs[2 * i + 1][...] = nt(
                ones, jnp.concatenate([prod[rows], fill], axis=0), precision=HIGH
            )


def forward(place, blocks, owns, quarters, after, w_gate, w_up, w_down):
    hidden = w_gate.shape[2]
    width = w_gate.shape[1] // EXPERTS
    count = len(quarters)
    split = len(blocks) - count
    slices = [lambda e: e] * count
    if split:
        slices[-1:] = [
            lambda e: jnp.minimum(e, AHEAD - 1),
            lambda e: jnp.maximum(e - AHEAD, 0),
        ]

    def tok_spec(at):
        return pl.BlockSpec((1, CAP, width), lambda e, _: (at(e), 0, 0))

    def og_spec(at):
        return pl.BlockSpec((1, CAP, WHOLE), lambda e, _: (at(e), 0, width // WHOLE))

    def own_spec(column):
        return pl.BlockSpec((1, CAP, PART), lambda e, _: (e, 0, column))

    in_specs = [tok_spec(at) for at in slices] + [og_spec(at) for at in slices]
    in_specs += [own_spec(a.shape[2] // PART - 1) for a in owns]
    operands = []

    def quarter_spec(index):
        return pl.BlockSpec((1, 1, CAP, PART), lambda e, at: (index, e, 0, 0))

    for index, arrays in quarters:
        in_specs += [quarter_spec(index)] * 3
        operands += arrays
    in_specs += [pl.BlockSpec(memory_space=pl.ANY)] * len(after)
    in_specs += [
        pl.BlockSpec((1, width, hidden), lambda e, at: (0, e, 0)),
        pl.BlockSpec((1, width, hidden), lambda e, at: (0, e, 0)),
        pl.BlockSpec((1, hidden, width), lambda e, at: (0, 0, e)),
    ]
    rows = count * CAP
    outs = pl.pallas_call(
        functools.partial(forward_kernel, count, split, len(after)),
        grid_spec=pltpu.PrefetchScalarGridSpec(
            num_scalar_prefetch=1,
            grid=(EXPERTS,),
            in_specs=in_specs,
            out_specs=[
                pl.BlockSpec((CAP, 2 * hidden), lambda e, at: (0, 0)),
                pl.BlockSpec((16, 128), lambda e, at: (0, 0)),
            ]
            * count,
            scratch_shapes=[pltpu.VMEM((rows, hidden), F32)] * 3 + [pltpu.VMEM((rows, width), BF)],
        ),
        out_shape=[
            jax.ShapeDtypeStruct((CAP, 2 * hidden), BF),
            jax.ShapeDtypeStruct((16, 128), F32),
        ]
        * count,
        compiler_params=pltpu.CompilerParams(vmem_limit_bytes=24 << 20),
        cost_estimate=pl.CostEstimate(
            flops=6 * 256 * EXPERTS * width * hidden,
            bytes_accessed=6 * EXPERTS * width * hidden,
            transcendentals=0,
        ),
        name="forward",
    )(place, *blocks, *blocks, *owns, *operands, *after, w_gate, w_up, w_down)
    return [(outs[2 * i], outs[2 * i + 1]) for i in range(count)]


def pack_slots(total, width):
    high = total.astype(BF).astype(F32)
    low = total - high
    row = lax.broadcasted_iota(jnp.int32, (16, 128), 0)
    packed = jnp.where(row == 0, high, jnp.where(row == 1, low, 0.0)).astype(BF)
    return jnp.concatenate([packed, jnp.zeros((16, width - 128), BF)], axis=1)


def unpack_slots(rows):
    packed = rows.astype(F32)
    return packed[0:1] + packed[1:2]


def product(grads, wg_ref, wu_ref, e):
    hidden = wg_ref.shape[2]
    width = wg_ref.shape[1] // EXPERTS
    part = pl.ds(pl.multiple_of(e * width, width), width)
    return nt(grads[:, :hidden], wg_ref[0, part, :]) + nt(grads[:, hidden:], wu_ref[0, part, :])


def backward_kernel(ways, got, first, wg_ref, wu_ref, *refs):
    grads, slots, received, outs = (refs[i * ways : (i + 1) * ways] for i in range(4))
    if not got:
        outs = received
    skip = 0 if first else 16
    if not first:
        for i in range(ways):
            total = slots[i][0:1, :]
            if got:
                total = total + unpack_slots(received[i][0:16, 0:128])
            outs[i][0:16, :] = pack_slots(total, outs[i].shape[1])
    rows_of = jnp.concatenate([r[...] for r in grads], axis=0)

    @pl.loop(0, EXPERTS // 2)
    def _(e):
        part = product(rows_of, wg_ref, wu_ref, first + e)
        rows = pl.ds(pl.multiple_of(skip + e * CAP, 16), CAP)
        for i in range(ways):
            own = part[i * CAP : (i + 1) * CAP]
            if got:
                own = own + received[i][rows, :].astype(F32)
            outs[i][rows, :] = own.astype(BF)


def backward(first, small, received, w_gate, w_up):
    hidden = w_gate.shape[2]
    width = w_gate.shape[1] // EXPERTS
    ways = len(small)
    rows = CAP * EXPERTS // 2 + (0 if first else 16)
    operands = [w_gate, w_up, *[a for a, _ in small], *[a for _, a in small], *received]
    return pl.pallas_call(
        functools.partial(backward_kernel, ways, bool(received), first),
        in_specs=[pl.BlockSpec(memory_space=pltpu.VMEM)] * len(operands),
        out_shape=[jax.ShapeDtypeStruct((rows, width), BF)] * ways,
        compiler_params=pltpu.CompilerParams(vmem_limit_bytes=24 << 20),
        cost_estimate=pl.CostEstimate(
            flops=2 * 256 * EXPERTS * width * hidden,
            bytes_accessed=2 * EXPERTS * width * hidden,
            transcendentals=0,
        ),
        name="backward",
    )(*operands)


def own_kernel(g_ref, wg_ref, wu_ref, out_ref):
    grads = g_ref[...]

    @pl.loop(0, EXPERTS)
    def _(e):
        out_ref[e] = product(grads, wg_ref, wu_ref, e)


def own_product(grads, w_gate, w_up):
    hidden = w_gate.shape[2]
    width = w_gate.shape[1] // EXPERTS
    return pl.pallas_call(
        own_kernel,
        in_specs=[pl.BlockSpec(memory_space=pltpu.VMEM)] * 3,
        out_shape=jax.ShapeDtypeStruct((EXPERTS, CAP, width), F32),
        compiler_params=pltpu.CompilerParams(vmem_limit_bytes=24 << 20),
        cost_estimate=pl.CostEstimate(
            flops=2 * 256 * EXPERTS * width * hidden,
            bytes_accessed=4 * EXPERTS * width * hidden,
            transcendentals=0,
        ),
        name="own_product",
    )(grads, w_gate, w_up)


def last_kernel(own_ref, s_ref, *refs):
    low, high, out_ref = refs[0:2], refs[2:4], refs[4]
    half = EXPERTS // 2
    total = s_ref[0:1, :] + (unpack_slots(low[0][0:16, 0:128]) + unpack_slots(low[1][0:16, 0:128]))
    width = own_ref.shape[2]
    row = lax.broadcasted_iota(jnp.int32, (CAP, 128), 0)
    column = lax.broadcasted_iota(jnp.int32, (CAP, 128), 1)
    total = jnp.sum(jnp.where(row == column, total, 0.0), axis=1, keepdims=True)
    high_part = total.astype(BF).astype(F32)
    tail = jnp.where(column == 0, high_part, jnp.where(column == 1, total - high_part, 0.0))
    tail = tail.astype(BF)
    for e in range(EXPERTS):
        parts, start = (low, 16 + e * CAP) if e < half else (high, (e - half) * CAP)
        rows = slice(start, start + CAP)
        sums = parts[0][rows, :].astype(F32) + parts[1][rows, :].astype(F32)
        out_ref[e, :, 0:width] = (own_ref[e] + sums).astype(BF)
        out_ref[e, :, width:] = tail


def last(own, slots, low, high):
    operands = [own, slots, *low, *high]
    return pl.pallas_call(
        last_kernel,
        in_specs=[pl.BlockSpec(memory_space=pltpu.VMEM)] * len(operands),
        out_shape=jax.ShapeDtypeStruct((EXPERTS, CAP, own.shape[2] + 128), BF),
        compiler_params=pltpu.CompilerParams(vmem_limit_bytes=24 << 20),
        name="last",
    )(*operands)


def combine_kernel(ids_ref, weight_ref, rows_ref, out_ref):
    ind0, ind1, count = slot_masks(ids_ref[...])
    tokens = ind0.shape[1]
    width = rows_ref.shape[2] - 128
    weights = weight_ref[...]
    scale = ind0 * weights[0:1, :] + ind1 * weights[1:2, :]
    slots = lax.broadcasted_iota(jnp.int32, (CAP, tokens), 0)
    picks = []
    ones0, ones1 = [], []
    for e in range(EXPERTS):
        here = count[e : e + 1, :] == slots
        picks.append(jnp.where(here, scale[e : e + 1, :], 0.0))
        ones0.append(jnp.where(here, ind0[e : e + 1, :], 0.0).astype(BF))
        ones1.append(jnp.where(here, ind1[e : e + 1, :], 0.0).astype(BF))
    sums = jnp.concatenate([rows_ref[e, :, width:] for e in range(EXPERTS)], axis=0)
    router0 = tn(sums, jnp.concatenate(ones0, axis=0))
    router1 = tn(sums, jnp.concatenate(ones1, axis=0))
    rest = jnp.concatenate(picks, axis=0)
    rows = jnp.concatenate([rows_ref[e, :, 0:width] for e in range(EXPERTS)], axis=0)
    total = jnp.zeros((tokens, width), F32)
    for _ in range(3):
        part = rest.astype(BF)
        total += tn(part, rows)
        rest = rest - part.astype(F32)
    out_ref[0:tokens, :] = total.astype(BF)
    sum0 = router0[0:1] + router0[1:2]
    sum1 = router1[0:1] + router1[1:2]
    high0, high1 = sum0.astype(BF).astype(F32), sum1.astype(BF).astype(F32)
    row = lax.broadcasted_iota(jnp.int32, (16, tokens), 0)
    packed = jnp.where(row == 0, high0, 0.0) + jnp.where(row == 1, sum0 - high0, 0.0)
    packed = packed + jnp.where(row == 2, high1, 0.0) + jnp.where(row == 3, sum1 - high1, 0.0)
    out_ref[tokens : tokens + 16, :] = jnp.concatenate(
        [packed.astype(BF), jnp.zeros((16, width - tokens), BF)], axis=1
    )


def combine(ids, weights, rows):
    tokens = ids.shape[1]
    return pl.pallas_call(
        combine_kernel,
        out_shape=jax.ShapeDtypeStruct((tokens + 16, rows.shape[2] - 128), BF),
        compiler_params=pltpu.CompilerParams(vmem_limit_bytes=24 << 20),
        name="combine",
    )(ids, weights, rows)


def finish_kernel(a_ref, b_ref, c_ref, d_ref, x_ref, r_ref):
    tokens = x_ref.shape[0]
    total = (a_ref[...].astype(F32) + c_ref[...].astype(F32)) + (
        b_ref[...].astype(F32) + d_ref[...].astype(F32)
    )
    x_ref[...] = total[:tokens].astype(BF)
    tail = total[tokens : tokens + 16, :tokens]
    r_ref[0:1, :] = tail[0:1] + tail[1:2]
    r_ref[1:2, :] = tail[2:3] + tail[3:4]


def finish(own, plus, two, minus):
    tokens = own.shape[0] - 16
    return pl.pallas_call(
        finish_kernel,
        out_shape=(
            jax.ShapeDtypeStruct((tokens, own.shape[1]), BF),
            jax.ShapeDtypeStruct((2, tokens), F32),
        ),
        compiler_params=pltpu.CompilerParams(vmem_limit_bytes=24 << 20),
        name="finish",
    )(own, plus, two, minus)


def shift(a, axis, by):
    n = lax.axis_size(axis)
    return lax.ppermute(a, axis, [(i, (i + by) % n) for i in range(n)])


def per_device(tokens, out_grad, expert_ids, combine_weights, w_gate, w_up, w_down):
    ids = expert_ids.T
    weights = combine_weights.T
    half = EXPERTS // 2
    place = lax.axis_index("tensor").astype(jnp.int32)[None]
    own = dispatch(place, ids, tokens, out_grad)
    own = lax.all_to_all(own, "expert", split_axis=0, concat_axis=0)

    width = own.shape[2] - PART
    blocks = {0: own}
    owns = {4: shift(own[:, :, width:], "dp", 4)}
    quarters = {}

    def spread(*dists):
        mine = jnp.concatenate([owns[d][:, :, -PART:] for d in dists], axis=0)
        others = [shift(mine, "tensor", by) for by in (1, -1, 2)]
        shaped = [a.reshape(len(dists), EXPERTS, CAP, PART) for a in others]
        quarters.update({d: (i, shaped) for i, d in enumerate(dists)})
        return others

    def hop(dist, beside):
        ahead, behind, *_ = lax.optimization_barrier((blocks[dist - 1], blocks[1 - dist], *beside))
        owns[dist] = blocks[dist] = shift(ahead, "dp", -1)
        owns[-dist] = blocks[-dist] = shift(behind, "dp", 1)

    owns[0] = own
    hop(1, [])
    hop(2, [owns[4]])
    hop(3, spread(0, 4))
    beside = spread(1, -1, 2, -2)
    low, high, *_ = lax.optimization_barrier(
        (blocks[-3][:AHEAD, :, :width], blocks[3][AHEAD:, :, :width], *beside)
    )
    split = [shift(low, "dp", 1), shift(high, "dp", -1)]
    spread(3, -3)

    grads = {}
    for dists in ((0, 1, -1, 2, -2), (3, -3, 4)):
        arrays = [blocks[d] for d in dists if d != 4] + (split if 4 in dists else [])
        found = forward(
            place,
            arrays,
            [owns[d] for d in dists],
            [quarters[d] for d in dists],
            [a for _, a in grads.values()][:1],
            w_gate,
            w_up,
            w_down,
        )
        grads.update(zip(dists, found))

    got = {0: (), half: ()}
    final = {0: {}, half: {}}
    for step in range(4):
        for first in ((0, half) if step % 2 == 0 else (half, 0)):
            long = 1 if first == 0 else -1
            dists = [long * (4 - step)] + ([-long * (3 - step)] if step < 3 else [])
            small = [grads[4 if d == -4 else d] for d in dists]
            received = got[first][: len(dists)]
            outs = backward(first, small, received, w_gate, w_up)
            sent = [shift(o, "dp", 1 if d > 0 else -1) for o, d in zip(outs, dists)]
            got[first] = sent
            final[first].update({i: a for i, a in enumerate(sent)})
    low = [final[0][0], final[0][1]]
    high = [final[half][0], final[half][1]]
    rows = last(own_product(grads[0][0], w_gate, w_up), grads[0][1], low, high)
    rows = lax.all_to_all(rows, "expert", split_axis=0, concat_axis=0)
    part = combine(ids, weights, rows)
    x_grad, router = finish(
        part, shift(part, "tensor", 1), shift(part, "tensor", 2), shift(part, "tensor", -1)
    )
    return x_grad, router.T


def solution(mesh):
    placed = (
        P("dp", "expert"),
        P("dp", "expert"),
        P("dp", None),
        P("dp", None),
        P("expert", None, ("dp", "tensor")),
        P("expert", None, ("dp", "tensor")),
        P("expert", ("dp", "tensor"), None),
    )
    return jax.shard_map(
        per_device,
        mesh=mesh,
        in_specs=placed,
        out_specs=(P("dp", "expert"), P("dp", None)),
        check_vma=False,
    )
```

```python
import functools

import jax
import jax.numpy as jnp
from jax import lax
from jax.experimental import pallas as pl
from jax.experimental.pallas import tpu as pltpu
from jax.sharding import PartitionSpec as P

EXPERTS = 8
CAP = 48
WHOLE = 256
PART = 128
AHEAD = 4
BF = jnp.bfloat16
F32 = jnp.float32
HIGH = lax.Precision.HIGHEST


def nt(a, b, **kw):
    return lax.dot_general(a, b, (((1,), (1,)), ((), ())), preferred_element_type=F32, **kw)


def tn(a, b, **kw):
    return lax.dot_general(a, b, (((0,), (0,)), ((), ())), preferred_element_type=F32, **kw)


def slot_masks(ids):
    tokens = ids.shape[1]
    experts = lax.broadcasted_iota(jnp.int32, (EXPERTS, tokens), 0)
    ind0 = (ids[0:1, :] == experts).astype(F32)
    ind1 = (ids[1:2, :] == experts).astype(F32)
    before = (
        lax.broadcasted_iota(jnp.int32, (tokens, tokens), 0)
        < lax.broadcasted_iota(jnp.int32, (tokens, tokens), 1)
    )
    count = jnp.dot((ind0 + ind1).astype(BF), before.astype(BF), preferred_element_type=F32)
    return ind0, ind1, count.astype(jnp.int32)


def dispatch_kernel(place_ref, ids_ref, tok_ref, og_ref, out_ref):
    ind0, ind1, count = slot_masks(ids_ref[...])
    ind = ind0 + ind1
    tokens = ind.shape[1]
    slots = lax.broadcasted_iota(jnp.int32, (CAP, tokens), 0)
    quarter = pl.ds(pl.multiple_of(WHOLE + place_ref[0] * PART, 128), PART)
    og = jnp.concatenate([og_ref[:, 0:WHOLE], og_ref[:, quarter]], axis=1)
    for e in range(EXPERTS):
        pick = jnp.where(count[e : e + 1, :] == slots, ind[e : e + 1, :], 0.0).astype(BF)
        width = tok_ref.shape[1]
        out_ref[e, :, :width] = jnp.dot(
            pick, tok_ref[...], preferred_element_type=F32
        ).astype(BF)
        out_ref[e, :, width:] = jnp.dot(pick, og, preferred_element_type=F32).astype(BF)


def dispatch(place, ids, tokens, out_grad):
    width = tokens.shape[1]
    return pl.pallas_call(
        dispatch_kernel,
        in_specs=[pl.BlockSpec(memory_space=pltpu.SMEM)]
        + [pl.BlockSpec(memory_space=pltpu.VMEM)] * 3,
        out_shape=jax.ShapeDtypeStruct((EXPERTS, CAP, width + WHOLE + PART), BF),
        compiler_params=pltpu.CompilerParams(vmem_limit_bytes=24 << 20),
        name="dispatch",
    )(place, ids, tokens, out_grad)


def forward_kernel(count, split, n_after, place_ref, *refs):
    toks, ogs = refs[: count + split], refs[count + split : 2 * (count + split)]
    refs = refs[2 * (count + split) :]
    owns = refs[:count]
    quarters = [refs[count + 3 * i : count + 3 * i + 3] for i in range(count)]
    refs = refs[4 * count + n_after :]
    wg_ref, wu_ref, wd_ref = refs[:3]
    outs = refs[3 : 3 + 2 * count]
    acc_g, acc_u, acc_b, og_ref = refs[3 + 2 * count :]
    e = pl.program_id(0)

    @pl.when(e == 0)
    def _():
        acc_g[...] = jnp.zeros_like(acc_g)
        acc_u[...] = jnp.zeros_like(acc_u)
        acc_b[...] = jnp.zeros_like(acc_b)

    tok, og = [r[0] for r in toks[:count]], [r[0] for r in ogs[:count]]
    if split:
        tok[-1] = jnp.where(e < AHEAD, tok[-1], toks[count][0])
        og[-1] = jnp.where(e < AHEAD, og[-1], ogs[count][0])
    tok = jnp.concatenate(tok, axis=0)
    for i in range(count):
        rows = slice(i * CAP, (i + 1) * CAP)
        og_ref[rows, 0:WHOLE] = og[i]
        pieces = [owns[i][0], *[r[0, 0] for r in quarters[i]]]
        for piece, offset in zip(pieces, (0, 3, 1, 2)):
            there = lax.rem(place_ref[0] + offset, 4)
            og_ref[rows, pl.ds(pl.multiple_of(WHOLE + there * PART, 128), PART)] = piece
    acc_g[...] += jnp.dot(tok, wg_ref[0], preferred_element_type=F32)
    acc_u[...] += jnp.dot(tok, wu_ref[0], preferred_element_type=F32)
    acc_b[...] += nt(og_ref[...], wd_ref[0])

    @pl.when(e == EXPERTS - 1)
    def _():
        gate, up, back = acc_g[...], acc_u[...], acc_b[...]
        sig = jax.nn.sigmoid(gate)
        act = gate * sig
        prod = back * (act * up)
        grad_up = (back * act).astype(BF)
        grad_gate = (back * up * sig * (1.0 + gate * (1.0 - sig))).astype(BF)
        hidden = gate.shape[1]
        ones = jnp.ones((16, hidden), F32)
        fill = jnp.zeros((128 - CAP, hidden), F32)
        for i in range(count):
            rows = slice(i * CAP, (i + 1) * CAP)
            outs[2 * i][:, :hidden] = grad_gate[rows]
            outs[2 * i][:, hidden:] = grad_up[rows]
            outs[2 * i + 1][...] = nt(
                ones, jnp.concatenate([prod[rows], fill], axis=0), precision=HIGH
            )


def forward(place, blocks, owns, quarters, after, w_gate, w_up, w_down):
    hidden = w_gate.shape[2]
    width = w_gate.shape[1] // EXPERTS
    count = len(quarters)
    split = len(blocks) - count
    slices = [lambda e: e] * count
    if split:
        slices[-1:] = [
            lambda e: jnp.minimum(e, AHEAD - 1),
            lambda e: jnp.maximum(e - AHEAD, 0),
        ]

    def tok_spec(at):
        return pl.BlockSpec((1, CAP, width), lambda e, _: (at(e), 0, 0))

    def og_spec(at):
        return pl.BlockSpec((1, CAP, WHOLE), lambda e, _: (at(e), 0, width // WHOLE))

    def own_spec(column):
        return pl.BlockSpec((1, CAP, PART), lambda e, _: (e, 0, column))

    in_specs = [tok_spec(at) for at in slices] + [og_spec(at) for at in slices]
    in_specs += [own_spec(a.shape[2] // PART - 1) for a in owns]
    operands = []

    def quarter_spec(index):
        return pl.BlockSpec((1, 1, CAP, PART), lambda e, at: (index, e, 0, 0))

    for index, arrays in quarters:
        in_specs += [quarter_spec(index)] * 3
        operands += arrays
    in_specs += [pl.BlockSpec(memory_space=pl.ANY)] * len(after)
    in_specs += [
        pl.BlockSpec((1, width, hidden), lambda e, at: (0, e, 0)),
        pl.BlockSpec((1, width, hidden), lambda e, at: (0, e, 0)),
        pl.BlockSpec((1, hidden, width), lambda e, at: (0, 0, e)),
    ]
    rows = count * CAP
    outs = pl.pallas_call(
        functools.partial(forward_kernel, count, split, len(after)),
        grid_spec=pltpu.PrefetchScalarGridSpec(
            num_scalar_prefetch=1,
            grid=(EXPERTS,),
            in_specs=in_specs,
            out_specs=[
                pl.BlockSpec((CAP, 2 * hidden), lambda e, at: (0, 0)),
                pl.BlockSpec((16, 128), lambda e, at: (0, 0)),
            ]
            * count,
            scratch_shapes=[pltpu.VMEM((rows, hidden), F32)] * 3 + [pltpu.VMEM((rows, width), BF)],
        ),
        out_shape=[
            jax.ShapeDtypeStruct((CAP, 2 * hidden), BF),
            jax.ShapeDtypeStruct((16, 128), F32),
        ]
        * count,
        compiler_params=pltpu.CompilerParams(vmem_limit_bytes=24 << 20),
        cost_estimate=pl.CostEstimate(
            flops=6 * 256 * EXPERTS * width * hidden,
            bytes_accessed=6 * EXPERTS * width * hidden,
            transcendentals=0,
        ),
        name="forward",
    )(place, *blocks, *blocks, *owns, *operands, *after, w_gate, w_up, w_down)
    return [(outs[2 * i], outs[2 * i + 1]) for i in range(count)]


def pack_slots(total, width):
    high = total.astype(BF).astype(F32)
    low = total - high
    row = lax.broadcasted_iota(jnp.int32, (16, 128), 0)
    packed = jnp.where(row == 0, high, jnp.where(row == 1, low, 0.0)).astype(BF)
    return jnp.concatenate([packed, jnp.zeros((16, width - 128), BF)], axis=1)


def unpack_slots(rows):
    packed = rows.astype(F32)
    return packed[0:1] + packed[1:2]


def product(grads, wg_ref, wu_ref, e):
    hidden = wg_ref.shape[2]
    width = wg_ref.shape[1] // EXPERTS
    part = pl.ds(pl.multiple_of(e * width, width), width)
    return nt(grads[:, :hidden], wg_ref[0, part, :]) + nt(grads[:, hidden:], wu_ref[0, part, :])


def backward_kernel(ways, got, first, wg_ref, wu_ref, *refs):
    grads, slots, received, outs = (refs[i * ways : (i + 1) * ways] for i in range(4))
    if not got:
        outs = received
    skip = 0 if first else 16
    if not first:
        for i in range(ways):
            total = slots[i][0:1, :]
            if got:
                total = total + unpack_slots(received[i][0:16, 0:128])
            outs[i][0:16, :] = pack_slots(total, outs[i].shape[1])
    rows_of = jnp.concatenate([r[...] for r in grads], axis=0)

    @pl.loop(0, EXPERTS // 2)
    def _(e):
        part = product(rows_of, wg_ref, wu_ref, first + e)
        rows = pl.ds(pl.multiple_of(skip + e * CAP, 16), CAP)
        for i in range(ways):
            own = part[i * CAP : (i + 1) * CAP]
            if got:
                own = own + received[i][rows, :].astype(F32)
            outs[i][rows, :] = own.astype(BF)


def backward(first, small, received, w_gate, w_up):
    hidden = w_gate.shape[2]
    width = w_gate.shape[1] // EXPERTS
    ways = len(small)
    rows = CAP * EXPERTS // 2 + (0 if first else 16)
    operands = [w_gate, w_up, *[a for a, _ in small], *[a for _, a in small], *received]
    return pl.pallas_call(
        functools.partial(backward_kernel, ways, bool(received), first),
        in_specs=[pl.BlockSpec(memory_space=pltpu.VMEM)] * len(operands),
        out_shape=[jax.ShapeDtypeStruct((rows, width), BF)] * ways,
        compiler_params=pltpu.CompilerParams(vmem_limit_bytes=24 << 20),
        cost_estimate=pl.CostEstimate(
            flops=2 * 256 * EXPERTS * width * hidden,
            bytes_accessed=2 * EXPERTS * width * hidden,
            transcendentals=0,
        ),
        name="backward",
    )(*operands)


def own_kernel(g_ref, wg_ref, wu_ref, out_ref):
    grads = g_ref[...]

    @pl.loop(0, EXPERTS)
    def _(e):
        out_ref[e] = product(grads, wg_ref, wu_ref, e)


def own_product(grads, w_gate, w_up):
    hidden = w_gate.shape[2]
    width = w_gate.shape[1] // EXPERTS
    return pl.pallas_call(
        own_kernel,
        in_specs=[pl.BlockSpec(memory_space=pltpu.VMEM)] * 3,
        out_shape=jax.ShapeDtypeStruct((EXPERTS, CAP, width), F32),
        compiler_params=pltpu.CompilerParams(vmem_limit_bytes=24 << 20),
        cost_estimate=pl.CostEstimate(
            flops=2 * 256 * EXPERTS * width * hidden,
            bytes_accessed=4 * EXPERTS * width * hidden,
            transcendentals=0,
        ),
        name="own_product",
    )(grads, w_gate, w_up)


def last_kernel(own_ref, s_ref, *refs):
    low, high, out_ref = refs[0:2], refs[2:4], refs[4]
    half = EXPERTS // 2
    total = s_ref[0:1, :] + (unpack_slots(low[0][0:16, 0:128]) + unpack_slots(low[1][0:16, 0:128]))
    width = own_ref.shape[2]
    row = lax.broadcasted_iota(jnp.int32, (CAP, 128), 0)
    column = lax.broadcasted_iota(jnp.int32, (CAP, 128), 1)
    total = jnp.sum(jnp.where(row == column, total, 0.0), axis=1, keepdims=True)
    high_part = total.astype(BF).astype(F32)
    tail = jnp.where(column == 0, high_part, jnp.where(column == 1, total - high_part, 0.0))
    tail = tail.astype(BF)
    for e in range(EXPERTS):
        parts, start = (low, 16 + e * CAP) if e < half else (high, (e - half) * CAP)
        rows = slice(start, start + CAP)
        sums = parts[0][rows, :].astype(F32) + parts[1][rows, :].astype(F32)
        out_ref[e, :, 0:width] = (own_ref[e] + sums).astype(BF)
        out_ref[e, :, width:] = tail


def last(own, slots, low, high):
    operands = [own, slots, *low, *high]
    return pl.pallas_call(
        last_kernel,
        in_specs=[pl.BlockSpec(memory_space=pltpu.VMEM)] * len(operands),
        out_shape=jax.ShapeDtypeStruct((EXPERTS, CAP, own.shape[2] + 128), BF),
        compiler_params=pltpu.CompilerParams(vmem_limit_bytes=24 << 20),
        name="last",
    )(*operands)


def combine_kernel(ids_ref, weight_ref, rows_ref, out_ref):
    ind0, ind1, count = slot_masks(ids_ref[...])
    tokens = ind0.shape[1]
    width = rows_ref.shape[2] - 128
    weights = weight_ref[...]
    scale = ind0 * weights[0:1, :] + ind1 * weights[1:2, :]
    slots = lax.broadcasted_iota(jnp.int32, (CAP, tokens), 0)
    picks = []
    ones0, ones1 = [], []
    for e in range(EXPERTS):
        here = count[e : e + 1, :] == slots
        picks.append(jnp.where(here, scale[e : e + 1, :], 0.0))
        ones0.append(jnp.where(here, ind0[e : e + 1, :], 0.0).astype(BF))
        ones1.append(jnp.where(here, ind1[e : e + 1, :], 0.0).astype(BF))
    sums = jnp.concatenate([rows_ref[e, :, width:] for e in range(EXPERTS)], axis=0)
    router0 = tn(sums, jnp.concatenate(ones0, axis=0))
    router1 = tn(sums, jnp.concatenate(ones1, axis=0))
    rest = jnp.concatenate(picks, axis=0)
    rows = jnp.concatenate([rows_ref[e, :, 0:width] for e in range(EXPERTS)], axis=0)
    total = jnp.zeros((tokens, width), F32)
    for _ in range(3):
        part = rest.astype(BF)
        total += tn(part, rows)
        rest = rest - part.astype(F32)
    out_ref[0:tokens, :] = total.astype(BF)
    sum0 = router0[0:1] + router0[1:2]
    sum1 = router1[0:1] + router1[1:2]
    high0, high1 = sum0.astype(BF).astype(F32), sum1.astype(BF).astype(F32)
    row = lax.broadcasted_iota(jnp.int32, (16, tokens), 0)
    packed = jnp.where(row == 0, high0, 0.0) + jnp.where(row == 1, sum0 - high0, 0.0)
    packed = packed + jnp.where(row == 2, high1, 0.0) + jnp.where(row == 3, sum1 - high1, 0.0)
    out_ref[tokens : tokens + 16, :] = jnp.concatenate(
        [packed.astype(BF), jnp.zeros((16, width - tokens), BF)], axis=1
    )


def combine(ids, weights, rows):
    tokens = ids.shape[1]
    return pl.pallas_call(
        combine_kernel,
        out_shape=jax.ShapeDtypeStruct((tokens + 16, rows.shape[2] - 128), BF),
        compiler_params=pltpu.CompilerParams(vmem_limit_bytes=24 << 20),
        name="combine",
    )(ids, weights, rows)


def finish_kernel(a_ref, b_ref, c_ref, d_ref, x_ref, r_ref):
    tokens = x_ref.shape[0]
    total = (a_ref[...].astype(F32) + c_ref[...].astype(F32)) + (
        b_ref[...].astype(F32) + d_ref[...].astype(F32)
    )
    x_ref[...] = total[:tokens].astype(BF)
    tail = total[tokens : tokens + 16, :tokens]
    r_ref[0:1, :] = tail[0:1] + tail[1:2]
    r_ref[1:2, :] = tail[2:3] + tail[3:4]


def finish(own, plus, two, minus):
    tokens = own.shape[0] - 16
    return pl.pallas_call(
        finish_kernel,
        out_shape=(
            jax.ShapeDtypeStruct((tokens, own.shape[1]), BF),
            jax.ShapeDtypeStruct((2, tokens), F32),
        ),
        compiler_params=pltpu.CompilerParams(vmem_limit_bytes=24 << 20),
        name="finish",
    )(own, plus, two, minus)


def shift(a, axis, by):
    n = lax.axis_size(axis)
    return lax.ppermute(a, axis, [(i, (i + by) % n) for i in range(n)])


def per_device(tokens, out_grad, expert_ids, combine_weights, w_gate, w_up, w_down):
    ids = expert_ids.T
    weights = combine_weights.T
    half = EXPERTS // 2
    place = lax.axis_index("tensor").astype(jnp.int32)[None]
    own = dispatch(place, ids, tokens, out_grad)
    own = lax.all_to_all(own, "expert", split_axis=0, concat_axis=0)

    width = own.shape[2] - PART
    blocks = {0: own}
    owns = {4: shift(own[:, :, width:], "dp", 4)}
    quarters = {}

    def spread(*dists):
        mine = jnp.concatenate([owns[d][:, :, -PART:] for d in dists], axis=0)
        others = [shift(mine, "tensor", by) for by in (1, -1, 2)]
        shaped = [a.reshape(len(dists), EXPERTS, CAP, PART) for a in others]
        quarters.update({d: (i, shaped) for i, d in enumerate(dists)})
        return others

    def hop(dist, beside):
        ahead, behind, *_ = lax.optimization_barrier((blocks[dist - 1], blocks[1 - dist], *beside))
        owns[dist] = blocks[dist] = shift(ahead, "dp", -1)
        owns[-dist] = blocks[-dist] = shift(behind, "dp", 1)

    owns[0] = own
    hop(1, [])
    hop(2, [])
    hop(3, spread(0, 4))
    beside = spread(1, -1, 2, -2)
    low, high, *_ = lax.optimization_barrier(
        (blocks[-3][:AHEAD, :, :width], blocks[3][AHEAD:, :, :width], *beside)
    )
    split = [shift(low, "dp", 1), shift(high, "dp", -1)]
    spread(3, -3)

    grads = {}
    for dists in ((0, 1, -1, 2, -2), (3, -3, 4)):
        arrays = [blocks[d] for d in dists if d != 4] + (split if 4 in dists else [])
        found = forward(
            place,
            arrays,
            [owns[d] for d in dists],
            [quarters[d] for d in dists],
            [a for _, a in grads.values()][:1],
            w_gate,
            w_up,
            w_down,
        )
        grads.update(zip(dists, found))

    got = {0: (), half: ()}
    final = {0: {}, half: {}}
    for step in range(4):
        for first in ((0, half) if step % 2 == 0 else (half, 0)):
            long = 1 if first == 0 else -1
            dists = [long * (4 - step)] + ([-long * (3 - step)] if step < 3 else [])
            small = [grads[4 if d == -4 else d] for d in dists]
            received = got[first][: len(dists)]
            outs = backward(first, small, received, w_gate, w_up)
            sent = [shift(o, "dp", 1 if d > 0 else -1) for o, d in zip(outs, dists)]
            got[first] = sent
            final[first].update({i: a for i, a in enumerate(sent)})
    low = [final[0][0], final[0][1]]
    high = [final[half][0], final[half][1]]
    rows = last(own_product(grads[0][0], w_gate, w_up), grads[0][1], low, high)
    rows = lax.all_to_all(rows, "expert", split_axis=0, concat_axis=0)
    part = combine(ids, weights, rows)
    x_grad, router = finish(
        part, shift(part, "tensor", 1), shift(part, "tensor", 2), shift(part, "tensor", -1)
    )
    return x_grad, router.T


def solution(mesh):
    placed = (
        P("dp", "expert"),
        P("dp", "expert"),
        P("dp", None),
        P("dp", None),
        P("expert", None, ("dp", "tensor")),
        P("expert", None, ("dp", "tensor")),
        P("expert", ("dp", "tensor"), None),
    )
    return jax.shard_map(
        per_device,
        mesh=mesh,
        in_specs=placed,
        out_specs=(P("dp", "expert"), P("dp", None)),
        check_vma=False,
    )
```
